32 devices in a mesh: sec: 2 (over y), row: 8 (over z, x), col: 2 (over core).
Axes of the slice: x: 2, y: 2, z: 4, core: 2. Of those that a mesh axis runs over, the one named last changes fastest.
Arguments:
- basis_matrix: bfloat16 [10240, 4096], P('row', 'col'), may hold values from -6 to 6
- operator_blocks: bfloat16 [80, 7, 128, 128], P('row', None, 'sec'), may hold values from -0.1875 to 0.1875
- neighbours: int32 [80, 7], P('row'), may hold values from 0 to 79, as said below
- neighbour_mask: int32 [80, 7], P('row'), may hold values from 0 to 1, as said below
Outputs:
- reduced: float32 [4096, 4096], P(('sec', 'row'), 'col')
The draws below stay inside these ranges and needn't reach their ends.
Inputs may be any that keep to these rules, and one draw needn't show every extreme that they name: `neighbours`: slot 0 of row block b is b; slots 1 to 4 are b - 1, b + 1, b - 2, b + 2; slots 5 and 6 lie within 2 blocks of b; a slot whose mask is 0 holds b. `neighbour_mask`: 0 exactly where slots 1 to 4 fall outside the slab, and at random in slots 5 and 6 (also where they fall outside); slot 0 is always 1.
All inputs are finite; a program needn't handle non-finite values.
Results may differ from the reference program's by a relative error of at most 0.0029.
Values may be sent and summed in bfloat16 or wider, within the bound.
No kernel may reach another device: no remote copies, remote signals or barrier semaphores. Data moves between devices by JAX's collectives and lax.ppermute only.
A program may use at most 192 MiB of HBM per device.

```python
import jax
import jax.numpy as jnp

K = 4096
BLOCK = 128
NEIGH = 7
REACH = 2
NB = 80
NODES = 10240


def neighbour_table(key):
    local_key = jax.random.fold_in(key, 7)
    first_key, second_key = jax.random.split(local_key)
    own_block = jnp.arange(NB, dtype=jnp.int32)[:, None]
    stencil = jnp.array([0, -1, 1, -REACH, REACH], dtype=jnp.int32)
    stencil_offsets = jnp.broadcast_to(stencil[None, :], (NB, 5))
    random_offsets = jax.random.randint(first_key, (NB, NEIGH - 5), -REACH, REACH + 1, dtype=jnp.int32)
    offsets = jnp.concatenate([stencil_offsets, random_offsets], axis=1)
    destination_rows = own_block + offsets
    inside = (destination_rows >= 0) & (destination_rows < NB)
    random_keep = jax.random.randint(second_key, (NB, NEIGH), 0, 4, dtype=jnp.int32) > 0
    kept_slot = jnp.where(jnp.arange(NEIGH)[None, :] < 5, True, random_keep)
    live_slot = inside & kept_slot
    return (jnp.where(live_slot, destination_rows, own_block).astype(jnp.int32), live_slot.astype(jnp.int32))


def draw_neighbours(key, part):
    return neighbour_table(key)[0]


def draw_neighbour_mask(key, part):
    return neighbour_table(key)[1]


def levels(rng, shape, cuts, low, high):
    factor_of, own = 1.0, jax.random.fold_in(rng, 6)
    for position, parts in cuts:
        draws = jnp.exp(jax.random.uniform(jax.random.fold_in(own, position), (parts,), jnp.float32, low / len(cuts), high / len(cuts)))
        factor_of = factor_of * jnp.repeat(draws, shape[position] // parts).reshape([-1 if axis == position else 1 for axis in range(len(shape))])
    return factor_of


def centred(key, extent, scale, most, cuts=(), held_as=jnp.bfloat16):
    gain = levels(key, extent, cuts, -0.22, 0.18) if cuts else 1.0
    values = jax.random.normal(key, extent, jnp.float32) * scale * gain
    return jnp.minimum(jnp.maximum(values, -most), most).astype(held_as)


def setup_inputs(seed: int = 0) -> dict:
    splits = jax.random.split(jax.random.key(seed), 5)
    return {
        "basis_matrix": centred(splits[0], (NODES, K), 1.0, 6.0, ((0, 8), (1, 2))),
        "operator_blocks": centred(splits[1], (NB, NEIGH, BLOCK, BLOCK), (NEIGH * BLOCK) ** -0.5, 0.1875, ((0, 8), (2, 2))),
        "neighbours": draw_neighbours(jax.random.fold_in(splits[4], 71), 0),
        "neighbour_mask": draw_neighbour_mask(jax.random.fold_in(splits[4], 71), 0),
    }


def reference(basis_matrix, operator_blocks, neighbours, neighbour_mask):
    block_count = operator_blocks.shape[0]
    reduced_basis_tiles = basis_matrix.reshape(block_count, BLOCK, K)
    applied_total_sum = jnp.zeros((block_count, BLOCK, K), jnp.float32)
    for neighbour in range(NEIGH):
        selected_entries = jnp.take(reduced_basis_tiles, neighbours[:, neighbour].astype(jnp.int32), axis=0).astype(jnp.float32)
        sparse_block_list = operator_blocks[:, neighbour].astype(jnp.float32)
        coupling_weight = neighbour_mask[:, neighbour].astype(jnp.float32)
        applied_total_sum = applied_total_sum + coupling_weight[:, None, None] * jnp.einsum('hol,hla->hoa', sparse_block_list, selected_entries)
    applied = applied_total_sum.astype(jnp.bfloat16).reshape(block_count * BLOCK, K)
    total = jnp.dot(basis_matrix.T, applied, preferred_element_type=jnp.float32)
    return total / jnp.sqrt(jnp.float32(NODES))
```

```python
import math

import jax
import jax.numpy as jnp
from jax import lax
from jax.experimental import pallas as pl
from jax.experimental.pallas import tpu as pltpu
from jax.sharding import PartitionSpec as P

REACH = 2
VMEM_LIMIT = 48 * 1024 * 1024


def apply_operator(basis, before, after, own_ops, other_ops, offsets, weights, order):
    rows, width = basis.shape
    blocks, slots, half, block = own_ops.shape
    rim = before.shape[0]
    tile = min(512, width)

    def kernel(off_ref, w_ref, order_ref, basis_ref, before_ref, after_ref, own_ref, other_ref, out_ref, ext):
        ext[pl.ds(0, rim), :] = before_ref[...]
        ext[pl.ds(rim, rows), :] = basis_ref[...]
        ext[pl.ds(rim + rows, rim), :] = after_ref[...]
        first = pl.multiple_of(order_ref[0] * half, half)
        second = pl.multiple_of((1 - order_ref[0]) * half, half)

        def body(b, carry):
            rhs = [
                ext[pl.ds(pl.multiple_of(off_ref[b, s] * block, block), block), :]
                for s in range(slots)
            ]
            lhs = [
                jnp.concatenate([own_ref[b, s], other_ref[b, s]], axis=0)
                * w_ref[b, s].astype(jnp.bfloat16)
                for s in range(slots)
            ]
            total = jnp.dot(
                jnp.concatenate(lhs, axis=1),
                jnp.concatenate(rhs, axis=0),
                preferred_element_type=jnp.float32,
            ).astype(jnp.bfloat16)
            base = pl.multiple_of(b * block, block)
            out_ref[pl.ds(base + first, half), :] = total[:half]
            out_ref[pl.ds(base + second, half), :] = total[half:]
            return carry

        lax.fori_loop(0, blocks, body, 0)

    return pl.pallas_call(
        kernel,
        grid_spec=pltpu.PrefetchScalarGridSpec(
            num_scalar_prefetch=3,
            grid=(width // tile,),
            in_specs=[
                pl.BlockSpec((rows, tile), lambda j, *_: (0, j)),
                pl.BlockSpec((rim, tile), lambda j, *_: (0, j)),
                pl.BlockSpec((rim, tile), lambda j, *_: (0, j)),
                pl.BlockSpec(own_ops.shape, lambda j, *_: (0, 0, 0, 0)),
                pl.BlockSpec(other_ops.shape, lambda j, *_: (0, 0, 0, 0)),
            ],
            out_specs=pl.BlockSpec((rows, tile), lambda j, *_: (0, j)),
            scratch_shapes=[pltpu.VMEM((rows + 2 * rim, tile), jnp.bfloat16)],
        ),
        out_shape=jax.ShapeDtypeStruct((rows, width), jnp.bfloat16),
        compiler_params=pltpu.CompilerParams(vmem_limit_bytes=VMEM_LIMIT),
        cost_estimate=pl.CostEstimate(
            flops=2 * rows * slots * block * width,
            bytes_accessed=2 * (2 * rows * width + 2 * rim * width + 2 * own_ops.size),
            transcendentals=0,
        ),
        name="apply_operator",
    )(offsets, weights, order, basis, before, after, own_ops, other_ops)


def tile_chunk(left, applied, chunk, height, addend, out_dtype):
    rows, width = applied.shape
    tile = min(512, width)

    def kernel(chunk_ref, left_ref, applied_ref, *rest):
        out_ref = rest[-1]
        total = lax.dot_general(
            left_ref[...], applied_ref[...], (((0,), (0,)), ((), ())),
            preferred_element_type=jnp.float32,
        )
        if len(rest) == 2:
            total = total + rest[0][...].astype(jnp.float32)
        out_ref[...] = total.astype(out_ref.dtype)

    in_specs = [
        pl.BlockSpec((rows, height), lambda j, c: (0, c[0])),
        pl.BlockSpec((rows, tile), lambda j, c: (0, j)),
    ]
    operands = [left, applied]
    if addend is not None:
        in_specs.append(pl.BlockSpec((height, tile), lambda j, c: (0, j)))
        operands.append(addend)
    return pl.pallas_call(
        kernel,
        grid_spec=pltpu.PrefetchScalarGridSpec(
            num_scalar_prefetch=1,
            grid=(width // tile,),
            in_specs=in_specs,
            out_specs=pl.BlockSpec((height, tile), lambda j, c: (0, j)),
        ),
        out_shape=jax.ShapeDtypeStruct((height, width), out_dtype),
        compiler_params=pltpu.CompilerParams(vmem_limit_bytes=VMEM_LIMIT),
        cost_estimate=pl.CostEstimate(
            flops=2 * rows * height * width,
            bytes_accessed=2 * rows * (height + width) + 6 * height * width,
            transcendentals=0,
        ),
        name="tile_chunk",
    )(chunk, left, applied, *([] if addend is None else [addend]))


def per_device(basis, own_ops, neighbours, mask):
    rows, width = basis.shape
    blocks, slots, half, block = own_ops.shape
    sec, row, col = (lax.axis_index(name) for name in ("sec", "row", "col"))
    count = lax.axis_size("row")
    rim = REACH * block

    up = [(i, i + 1) for i in range(count - 1)]
    down = [(i + 1, i) for i in range(count - 1)]
    before = lax.ppermute(basis[rows - rim:], "row", up)
    after = lax.ppermute(basis[:rim], "row", down)
    other_ops = lax.ppermute(own_ops, "sec", [(0, 1), (1, 0)])
    moved = lax.ppermute(basis, ("sec", "col"), [(0, 1), (3, 2)])
    left = jnp.where(sec == col, basis, moved)

    offsets = neighbours - row * blocks + REACH
    applied = apply_operator(
        basis, before, after, own_ops, other_ops, offsets,
        mask.astype(jnp.float32), sec.astype(jnp.int32)[None],
    )

    groups = count // 2
    group, side = row // 2, row % 2
    height = width * lax.axis_size("col") // lax.axis_size("sec") // count
    pack = min(groups, max(1, 256 // height))
    packs = groups // pack
    if pack > 1:
        left = left.reshape(rows, groups, 2, height).swapaxes(1, 2).reshape(rows, -1)

    def column_block(step, which):
        target = (group // pack + step) % packs
        return (2 * target + which if pack == 1 else which * packs + target)[None]

    swap = [(i, i ^ 1) for i in range(count)]
    steps = sorted(range(1, packs), key=lambda k: -min(k, packs - k)) + [0]

    sums = {}
    for step in steps:
        away = tile_chunk(
            left, applied, column_block(step, 1 - side), pack * height, None, jnp.bfloat16
        )
        sums[step] = lax.ppermute(away, "row", swap)
    total = None
    arrived = []
    for step in steps:
        mine = tile_chunk(
            left, applied, column_block(step, side), pack * height, sums[step],
            jnp.float32 if step == 0 else jnp.bfloat16,
        )
        for i in range(pack):
            part = mine
            if pack > 1:
                place = (group + i) % pack * height
                part = lax.dynamic_slice_in_dim(mine, place, height, axis=0)
            if step == 0 and i == 0:
                total = part
                continue
            route = []
            for g in range(groups):
                to = (g // pack + step) % packs * pack + (g + i) % pack
                route += [(2 * g, 2 * to), (2 * g + 1, 2 * to + 1)]
            arrived.append(lax.ppermute(part.astype(jnp.bfloat16), "row", route))
    for part in arrived:
        total = total + part.astype(jnp.float32)
    return total * (1.0 / math.sqrt(rows * count))


def solution(mesh):
    return jax.shard_map(
        per_device,
        mesh=mesh,
        in_specs=(P("row", "col"), P("row", None, "sec", None), P("row", None), P("row", None)),
        out_specs=P(("sec", "row"), "col"),
        check_vma=False,
    )
```

```python
import math

import jax
import jax.numpy as jnp
from jax import lax
from jax.experimental import pallas as pl
from jax.experimental.pallas import tpu as pltpu
from jax.sharding import PartitionSpec as P

REACH = 2
VMEM_LIMIT = 48 * 1024 * 1024


def apply_operator(basis, before, after, own_ops, other_ops, offsets, weights, order):
    rows, width = basis.shape
    blocks, slots, half, block = own_ops.shape
    rim = before.shape[0]
    tile = min(512, width)

    def kernel(off_ref, w_ref, order_ref, basis_ref, before_ref, after_ref, own_ref, other_ref, out_ref, ext):
        ext[pl.ds(0, rim), :] = before_ref[...]
        ext[pl.ds(rim, rows), :] = basis_ref[...]
        ext[pl.ds(rim + rows, rim), :] = after_ref[...]
        first = pl.multiple_of(order_ref[0] * half, half)
        second = pl.multiple_of((1 - order_ref[0]) * half, half)

        def body(b, carry):
            rhs = [
                ext[pl.ds(pl.multiple_of(off_ref[b, s] * block, block), block), :]
                for s in range(slots)
            ]
            lhs = [
                jnp.concatenate([own_ref[b, s], other_ref[b, s]], axis=0)
                * w_ref[b, s].astype(jnp.bfloat16)
                for s in range(slots)
            ]
            total = jnp.dot(
                jnp.concatenate(lhs, axis=1),
                jnp.concatenate(rhs, axis=0),
                preferred_element_type=jnp.float32,
            ).astype(jnp.bfloat16)
            base = pl.multiple_of(b * block, block)
            out_ref[pl.ds(base + first, half), :] = total[:half]
            out_ref[pl.ds(base + second, half), :] = total[half:]
            return carry

        lax.fori_loop(0, blocks, body, 0)

    return pl.pallas_call(
        kernel,
        grid_spec=pltpu.PrefetchScalarGridSpec(
            num_scalar_prefetch=3,
            grid=(width // tile,),
            in_specs=[
                pl.BlockSpec((rows, tile), lambda j, *_: (0, j)),
                pl.BlockSpec((rim, tile), lambda j, *_: (0, j)),
                pl.BlockSpec((rim, tile), lambda j, *_: (0, j)),
                pl.BlockSpec(own_ops.shape, lambda j, *_: (0, 0, 0, 0)),
                pl.BlockSpec(other_ops.shape, lambda j, *_: (0, 0, 0, 0)),
            ],
            out_specs=pl.BlockSpec((rows, tile), lambda j, *_: (0, j)),
            scratch_shapes=[pltpu.VMEM((rows + 2 * rim, tile), jnp.bfloat16)],
        ),
        out_shape=jax.ShapeDtypeStruct((rows, width), jnp.bfloat16),
        compiler_params=pltpu.CompilerParams(vmem_limit_bytes=VMEM_LIMIT),
        cost_estimate=pl.CostEstimate(
            flops=2 * rows * slots * block * width,
            bytes_accessed=2 * (2 * rows * width + 2 * rim * width + 2 * own_ops.size),
            transcendentals=0,
        ),
        name="apply_operator",
    )(offsets, weights, order, basis, before, after, own_ops, other_ops)


def tile_chunk(left, applied, chunk, height, addend, out_dtype):
    rows, width = applied.shape
    tile = min(512, width)

    def kernel(chunk_ref, left_ref, applied_ref, *rest):
        out_ref = rest[-1]
        total = lax.dot_general(
            left_ref[...], applied_ref[...], (((0,), (0,)), ((), ())),
            preferred_element_type=jnp.float32,
        )
        if len(rest) == 2:
            total = total + rest[0][...].astype(jnp.float32)
        out_ref[...] = total.astype(out_ref.dtype)

    in_specs = [
        pl.BlockSpec((rows, height), lambda j, c: (0, c[0])),
        pl.BlockSpec((rows, tile), lambda j, c: (0, j)),
    ]
    operands = [left, applied]
    if addend is not None:
        in_specs.append(pl.BlockSpec((height, tile), lambda j, c: (0, j)))
        operands.append(addend)
    return pl.pallas_call(
        kernel,
        grid_spec=pltpu.PrefetchScalarGridSpec(
            num_scalar_prefetch=1,
            grid=(width // tile,),
            in_specs=in_specs,
            out_specs=pl.BlockSpec((height, tile), lambda j, c: (0, j)),
        ),
        out_shape=jax.ShapeDtypeStruct((height, width), out_dtype),
        compiler_params=pltpu.CompilerParams(vmem_limit_bytes=VMEM_LIMIT),
        cost_estimate=pl.CostEstimate(
            flops=2 * rows * height * width,
            bytes_accessed=2 * rows * (height + width) + 6 * height * width,
            transcendentals=0,
        ),
        name="tile_chunk",
    )(chunk, left, applied, *([] if addend is None else [addend]))


def per_device(basis, own_ops, neighbours, mask):
    rows, width = basis.shape
    blocks, slots, half, block = own_ops.shape
    sec, row, col = (lax.axis_index(name) for name in ("sec", "row", "col"))
    count = lax.axis_size("row")
    rim = REACH * block

    up = [(i, i + 1) for i in range(count - 1)]
    down = [(i + 1, i) for i in range(count - 1)]
    before = lax.ppermute(basis[rows - rim:], "row", up)
    after = lax.ppermute(basis[:rim], "row", down)
    other_ops = lax.ppermute(own_ops, "sec", [(0, 1), (1, 0)])
    moved = lax.ppermute(basis, ("sec", "col"), [(0, 1), (3, 2)])
    left = jnp.where(sec == col, basis, moved)

    offsets = neighbours - row * blocks + REACH
    applied = apply_operator(
        basis, before, after, own_ops, other_ops, offsets,
        mask.astype(jnp.float32), sec.astype(jnp.int32)[None],
    )

    height = width * lax.axis_size("col") // lax.axis_size("sec") // count
    fars = count // 4
    far, pair, side = row // 4, row // 2 % 2, row % 2
    swap_side = [(i, i ^ 1) for i in range(count)]
    swap_pair = [(i, i ^ 2) for i in range(count)]

    def block(steps, pair, side, dtype):
        where = [((far + step) % fars * 2 + pair) * 2 + side for step in steps]
        if len(steps) == 1 and height % 128 == 0:
            return tile_chunk(left, applied, where[0][None], height, None, dtype)
        columns = [lax.dynamic_slice_in_dim(left, w * height, height, 1) for w in where]
        wide = -len(steps) * height % 128
        if wide:
            columns.append(jnp.zeros((rows, wide), left.dtype))
        made = tile_chunk(
            jnp.concatenate(columns, 1), applied, jnp.zeros((1,), jnp.int32),
            len(steps) * height + wide, None, dtype,
        )
        return made[: len(steps) * height]

    def add(first, *others):
        for other in others:
            first = first + other.astype(jnp.float32)
        return first

    away = list(range(1, fars))
    f32, bf16 = jnp.float32, jnp.bfloat16
    far_a = lax.ppermute(block(away, 1 - pair, 1 - side, bf16), "row", swap_side)
    near_a = lax.ppermute(block([0], 1 - pair, 1 - side, bf16), "row", swap_pair)
    far_b = lax.ppermute(block(away, pair, 1 - side, bf16), "row", swap_side)
    far_c = add(block(away, 1 - pair, side, f32), far_a).astype(bf16)
    far_c = lax.ppermute(far_c, "row", swap_pair)
    near_b = lax.ppermute(block([0], 1 - pair, side, bf16), "row", swap_pair)
    near_c = add(block([0], pair, 1 - side, f32), near_a).astype(bf16)
    near_c = lax.ppermute(near_c, "row", swap_side)
    far_d = add(block(away, pair, side, f32), far_b, far_c).astype(bf16)
    parts = []
    for i, step in enumerate(away):
        route = [(g, (g + 4 * step) % count) for g in range(count)]
        parts.append(lax.ppermute(far_d[i * height : (i + 1) * height], "row", route))
    total = add(block([0], pair, side, f32), near_b, near_c, *parts)
    return total * (1.0 / math.sqrt(rows * count))


def solution(mesh):
    return jax.shard_map(
        per_device,
        mesh=mesh,
        in_specs=(P("row", "col"), P("row", None, "sec", None), P("row", None), P("row", None)),
        out_specs=P(("sec", "row"), "col"),
        check_vma=False,
    )
```

```python
import math

import jax
import jax.numpy as jnp
from jax import lax
from jax.experimental import pallas as pl
from jax.experimental.pallas import tpu as pltpu
from jax.sharding import PartitionSpec as P

REACH = 2
BACK = (1, 3, 5, 6)
VMEM_LIMIT = 48 * 1024 * 1024
F32, BF16 = jnp.float32, jnp.bfloat16


def call(kernel, scalars, grid, in_specs, operands, out_spec, out_shape, scratch, flops, name):
    moved = sum(x.size * x.dtype.itemsize for x in operands)
    return pl.pallas_call(
        kernel,
        grid_spec=pltpu.PrefetchScalarGridSpec(
            num_scalar_prefetch=len(scalars), grid=grid, in_specs=in_specs,
            out_specs=out_spec, scratch_shapes=scratch,
        ),
        out_shape=out_shape,
        compiler_params=pltpu.CompilerParams(vmem_limit_bytes=VMEM_LIMIT),
        cost_estimate=pl.CostEstimate(flops=flops, bytes_accessed=moved, transcendentals=0),
        name=name,
    )(*scalars, *operands)


def apply_block(picks, halves, sec, rows_ref, out_ref, base):
    half, block = halves(picks[0][0])[0].shape
    rhs, lhs = [], []
    for slot, place, weight in picks:
        rhs.append(rows_ref[pl.ds(pl.multiple_of(place * block, block), block), :])
        lhs.append(jnp.concatenate(halves(slot), axis=0) * weight.astype(F32).astype(BF16))
    total = jnp.dot(
        jnp.concatenate(lhs, axis=1), jnp.concatenate(rhs, axis=0), preferred_element_type=F32
    ).astype(BF16)
    for i, place in enumerate((sec, 1 - sec)):
        start = pl.multiple_of(base + place * half, half)
        out_ref[pl.ds(start, half), :] = total[i * half : (i + 1) * half]


def apply_inner(basis, own_ops, share, rest, neighbours, mask, ids):
    rows, width = basis.shape
    blocks, slots, half, block = own_ops.shape
    inner, part = blocks - REACH, blocks // 2
    tile = min(512, width)

    def kernel(nb_ref, mask_ref, sec_ref, col_ref, row_ref, rows_ref, own_ref, share_ref, rest_ref, out_ref):
        first = row_ref[0] * blocks

        def body(b, carry):
            shared = b // part == col_ref[0]
            picks = []
            for s in range(slots):
                place = nb_ref[b, s] - first
                weight = jnp.where(place < 0, 0, mask_ref[b, s])
                picks.append((s, jnp.maximum(place, 0), weight))

            def halves(s):
                other = jnp.where(shared, share_ref[b % part, s], rest_ref[b % part, s])
                return own_ref[b, s], other

            apply_block(picks, halves, sec_ref[0], rows_ref, out_ref, b * block)
            return carry

        lax.fori_loop(0, inner, body, 0)

    share_spec = pl.BlockSpec(share.shape, lambda j, *_: (0, 0, 0, 0))
    return call(
        kernel, (neighbours, mask, *ids), (width // tile,),
        [pl.BlockSpec((rows, tile), lambda j, *_: (0, j)),
         pl.BlockSpec((inner, slots, half, block), lambda j, *_: (0, 0, 0, 0)),
         share_spec, share_spec],
        (basis, own_ops, share, rest),
        pl.BlockSpec((inner * block, tile), lambda j, *_: (0, j)),
        jax.ShapeDtypeStruct((inner * block, width), BF16), [],
        2 * inner * slots * block * block * width, "apply_inner",
    )


def apply_rim(basis, after, own_ops, share, rest, neighbours, mask, next_own, next_other,
              next_neighbours, next_mask, ids):
    rows, width = basis.shape
    blocks, slots, half, block = own_ops.shape
    rim, inner, part = REACH * block, blocks - REACH, blocks // 2
    base = blocks - 2 * REACH
    tile = min(512, width)

    def kernel(nb_ref, mask_ref, nnb_ref, nmask_ref, sec_ref, col_ref, row_ref, a_ref, b_ref, c_ref,
               own_ref, share_ref, rest_ref, next_ref, next_other_ref, out_ref, ext):
        first = row_ref[0] * blocks
        for i, ref in enumerate((a_ref, b_ref, c_ref)):
            ext[pl.ds(i * rim, rim), :] = ref[...]
        for i in range(REACH):
            picks = []
            for s in range(slots):
                place = nb_ref[inner + i, s] - first - base
                picks.append((s, jnp.maximum(place, 0), mask_ref[inner + i, s]))

            def halves(s, i=i):
                b = inner + i - part
                other = jnp.where(col_ref[0] == 1, share_ref[b, s], rest_ref[b, s])
                return own_ref[i, s], other

            apply_block(picks, halves, sec_ref[0], ext, out_ref, i * block)
        for i in range(REACH):
            picks = []
            for s in BACK:
                place = nnb_ref[i, s] - first - base
                weight = jnp.where(place < 2 * REACH, nmask_ref[i, s], 0)
                picks.append((s, jnp.clip(place, 0, 3 * REACH - 1), weight))

            def halves(s, i=i):
                return next_ref[i, s], next_other_ref[i, s]

            apply_block(picks, halves, sec_ref[0], ext, out_ref, rim + i * block)

    last = rows // rim - 1
    share_spec = pl.BlockSpec(share.shape, lambda j, *_: (0, 0, 0, 0))
    next_spec = pl.BlockSpec(next_own.shape, lambda j, *_: (0, 0, 0, 0))
    return call(
        kernel, (neighbours, mask, next_neighbours, next_mask, *ids), (width // tile,),
        [pl.BlockSpec((rim, tile), lambda j, *_: (last - 1, j)),
         pl.BlockSpec((rim, tile), lambda j, *_: (last, j)),
         pl.BlockSpec((rim, tile), lambda j, *_: (0, j)),
         pl.BlockSpec((REACH, slots, half, block), lambda j, *_: (inner // REACH, 0, 0, 0)),
         share_spec, share_spec] + [next_spec] * 2,
        (basis, basis, after, own_ops, share, rest, next_own, next_other),
        pl.BlockSpec((2 * rim, tile), lambda j, *_: (0, j)),
        jax.ShapeDtypeStruct((2 * rim, width), BF16),
        [pltpu.VMEM((3 * rim, tile), BF16)],
        2 * REACH * (slots + len(BACK)) * block * block * width, "apply_rim",
    )


def tile_chunk(terms, scalars, height, addend, dtype):
    width = terms[0][4].shape[1]
    tile = min(512, width)
    count = len(terms)

    def kernel(chunk_ref, mine_ref, *refs):
        out_ref = refs[-1]
        total = None if addend is None else refs[3 * count][...].astype(F32)
        for i in range(count):
            mine, moved, applied = refs[3 * i : 3 * i + 3]
            left = jnp.where(mine_ref[0] == 1, mine[...], moved[...])
            part = lax.dot_general(
                left, applied[...], (((0,), (0,)), ((), ())), preferred_element_type=F32
            )
            total = part if total is None else total + part
        out_ref[...] = total.astype(out_ref.dtype)

    in_specs, operands = [], []
    for mine, moved, first, rows, applied, place in terms:
        spec = pl.BlockSpec((rows, height), lambda j, c, m, first=first: (first, c[0]))
        in_specs += [spec, spec, pl.BlockSpec((rows, tile), lambda j, c, m, place=place: (place, j))]
        operands += [mine, moved, applied]
    out_spec = pl.BlockSpec((height, tile), lambda j, *_: (0, j))
    if addend is not None:
        in_specs.append(out_spec)
        operands.append(addend)
    return call(
        kernel, scalars, (width // tile,), in_specs, operands, out_spec,
        jax.ShapeDtypeStruct((height, width), dtype), [],
        2 * sum(t[3] for t in terms) * height * width, "tile_chunk",
    )


def per_device(basis, own_ops, neighbours, mask):
    rows, width = basis.shape
    blocks, slots, half, block = own_ops.shape
    sec, row, col = (lax.axis_index(name) for name in ("sec", "row", "col"))
    count = lax.axis_size("row")
    rim = REACH * block
    inner = blocks - REACH
    swap = [(0, 1), (1, 0)]
    down = [(i + 1, i) for i in range(count - 1)]
    to_other = [(0, 1), (3, 2)]

    part = blocks // 2
    share = lax.dynamic_slice_in_dim(own_ops, col * part, part, 0)
    behind, share = lax.optimization_barrier((basis, share))
    next_own = lax.ppermute(own_ops[:REACH], "row", down)
    after = lax.ppermute(basis[:rim], "row", down)
    share = lax.ppermute(share, "sec", swap)
    next_neighbours = lax.ppermute(neighbours, "row", down)
    next_mask = lax.ppermute(mask, "row", down)
    moved = lax.ppermute(behind, ("sec", "col"), to_other)
    share, next_own, next_neighbours, next_mask = lax.optimization_barrier(
        (share, next_own, next_neighbours, next_mask)
    )
    rest = lax.ppermute(share, "col", swap)
    next_other = lax.ppermute(next_own, "sec", swap)
    rest, next_other = lax.optimization_barrier((rest, next_other))

    ids = tuple(x.astype(jnp.int32)[None] for x in (sec, col, row))
    applied = apply_inner(basis, own_ops, share, rest, neighbours, mask, ids)
    after, applied = lax.optimization_barrier((after, applied))
    after_moved = lax.ppermute(after, ("sec", "col"), to_other)

    height = width * lax.axis_size("col") // lax.axis_size("sec") // count
    fars = count // 4
    far, pair, side = row // 4, row // 2 % 2, row % 2
    swap_side = [(i, i ^ 1) for i in range(count)]
    swap_pair = [(i, i ^ 2) for i in range(count)]
    is_mine = (sec == col).astype(jnp.int32)[None]

    def chunk(steps, pair, side, dtype, which="all", addend=None):
        where = [((far + step) % fars * 2 + pair) * 2 + side for step in steps]
        size = len(steps) * height
        lefts = [basis, moved, after, after_moved]
        if len(steps) == 1 and height % 128 == 0:
            index = where[0][None]
        else:
            index = jnp.zeros((1,), jnp.int32)
            fill = -size % 128
            size += fill
            lefts = [
                jnp.concatenate(
                    [lax.dynamic_slice_in_dim(x, w * height, height, 1) for w in where]
                    + [jnp.zeros((x.shape[0], fill), x.dtype)], 1)
                for x in lefts
            ]
        mine, other, mine_after, other_after = lefts
        terms = []
        if which != "rim":
            terms += [(mine, other, 0, inner * block, applied, 0)]
        if which != "inner":
            terms += [(mine, other, rows // rim - 1, rim, applied_rim, 0),
                      (mine_after, other_after, 0, rim, applied_rim, 1)]
        return tile_chunk(terms, (index, is_mine), size, addend, dtype)[: len(steps) * height]

    def add(first, *others):
        for other in others:
            first = first + other.astype(F32)
        return first

    away = list(range(1, fars))
    early = [chunk(away, 1 - pair, 1 - side, F32, "inner"), chunk([0], 1 - pair, 1 - side, F32, "inner")]
    *early, late = lax.optimization_barrier((*early, after))
    applied_rim = apply_rim(
        basis, late, own_ops, share, rest, neighbours, mask, next_own, next_other, next_neighbours,
        next_mask, ids
    )
    if height % 128 == 0:
        far_a = chunk(away, 1 - pair, 1 - side, BF16, "rim", early[0])
        near_a = chunk([0], 1 - pair, 1 - side, BF16, "rim", early[1])
    else:
        far_a = chunk(away, 1 - pair, 1 - side, BF16)
        near_a = chunk([0], 1 - pair, 1 - side, BF16)
    near_a, applied_rim = lax.optimization_barrier((near_a, applied_rim))
    far_a = lax.ppermute(far_a, "row", swap_side)
    near_a = lax.ppermute(near_a, "row", swap_pair)
    far_a, far_b = lax.optimization_barrier((far_a, chunk(away, pair, 1 - side, BF16)))
    far_b = lax.ppermute(far_b, "row", swap_side)
    far_c = add(chunk(away, 1 - pair, side, F32), far_a).astype(BF16)
    far_c = lax.ppermute(far_c, "row", swap_pair)
    near_b = lax.ppermute(chunk([0], 1 - pair, side, BF16), "row", swap_pair)
    near_c = add(chunk([0], pair, 1 - side, F32), near_a).astype(BF16)
    near_c = lax.ppermute(near_c, "row", swap_side)
    far_d = add(chunk(away, pair, side, F32), far_b, far_c).astype(BF16)
    parts = []
    for i, step in enumerate(away):
        route = [(g, (g + 4 * step) % count) for g in range(count)]
        parts.append(lax.ppermute(far_d[i * height : (i + 1) * height], "row", route))
    total = add(chunk([0], pair, side, F32), near_b, near_c, *parts)
    return total * (1.0 / math.sqrt(rows * count))


def solution(mesh):
    return jax.shard_map(
        per_device,
        mesh=mesh,
        in_specs=(P("row", "col"), P("row", None, "sec", None), P("row", None), P("row", None)),
        out_specs=P(("sec", "row"), "col"),
        check_vma=False,
    )
```

```python
import math

import jax
import jax.numpy as jnp
from jax import lax
from jax.experimental import pallas as pl
from jax.experimental.pallas import tpu as pltpu
from jax.sharding import PartitionSpec as P

REACH = 2
VMEM_LIMIT = 56 * 1024 * 1024
F32, BF16 = jnp.float32, jnp.bfloat16


def call(kernel, scalars, grid, in_specs, operands, out_specs, out_shape, scratch, flops, name):
    moved = sum(x.size * x.dtype.itemsize for x in operands)
    return pl.pallas_call(
        kernel,
        grid_spec=pltpu.PrefetchScalarGridSpec(
            num_scalar_prefetch=len(scalars), grid=grid, in_specs=in_specs,
            out_specs=out_specs, scratch_shapes=scratch,
        ),
        out_shape=out_shape,
        compiler_params=pltpu.CompilerParams(vmem_limit_bytes=VMEM_LIMIT),
        cost_estimate=pl.CostEstimate(flops=flops, bytes_accessed=moved, transcendentals=0),
        name=name,
    )(*scalars, *operands)


def fixed(array):
    return pl.BlockSpec(array.shape, lambda j, *_: (0,) * array.ndim)


def transposed_dot(left, right):
    return lax.dot_general(left, right, (((0,), (0,)), ((), ())), preferred_element_type=F32)


def apply_block(b, shift, nb_ref, mask_ref, sec, first, halves, rows_ref, out_ref, base):
    slots = nb_ref.shape[1]
    rhs, lhs = [], []
    for s in range(slots):
        own, other = halves(s)
        half, block = own.shape
        place = nb_ref[b, s] - first + shift
        rhs.append(rows_ref[pl.ds(pl.multiple_of(place * block, block), block), :])
        weight = mask_ref[b, s].astype(F32).astype(BF16)
        lhs.append(jnp.concatenate([own, other], axis=0) * weight)
    total = jnp.dot(
        jnp.concatenate(lhs, axis=1), jnp.concatenate(rhs, axis=0), preferred_element_type=F32
    ).astype(BF16)
    for i, half_of in enumerate((sec, 1 - sec)):
        start = pl.multiple_of(base + half_of * half, half)
        out_ref[pl.ds(start, half), :] = total[i * half : (i + 1) * half]


def inner_rows(basis, own_ops, share, rest, tables, ids, lefts, index, size):
    rows, width = basis.shape
    blocks, slots, half, block = own_ops.shape
    part, rim = blocks // 2, REACH * block
    tile = min(1024, width)

    def kernel(nb_ref, mask_ref, sec_ref, col_ref, row_ref, index_ref, rows_ref, own_ref, share_ref, rest_ref,
               m0, o0, m1, o1, out_ref, unit_ref):
        mine = sec_ref[0] == col_ref[0]
        for b in range(REACH, blocks - REACH):
            def halves(s, b=b):
                other = jnp.where(col_ref[0] == b // part, share_ref[b % part, s], rest_ref[b % part, s])
                return own_ref[b, s], other

            apply_block(b, 0, nb_ref, mask_ref, sec_ref[0], row_ref[0] * blocks, halves, rows_ref,
                        out_ref, (b - REACH) * block)
        for u, (here, there) in enumerate(((m0, o0), (m1, o1))):
            left = jnp.where(mine, here[rim : rows - rim, :], there[rim : rows - rim, :])
            unit_ref[u] = transposed_dot(left, out_ref[...])

    unit = [pl.BlockSpec((rows, size), lambda j, *s, u=u: (0, s[5][u])) for u in (0, 0, 1, 1)]
    return call(
        kernel, (*tables, *ids, index), (width // tile,),
        [pl.BlockSpec((rows, tile), lambda j, *_: (0, j)), fixed(own_ops), fixed(share), fixed(rest)] + unit,
        (basis, own_ops, share, rest, *lefts, *lefts),
        [pl.BlockSpec((rows - 2 * rim, tile), lambda j, *_: (0, j)),
         pl.BlockSpec((2, size, tile), lambda j, *_: (0, 0, j))],
        [jax.ShapeDtypeStruct((rows - 2 * rim, width), BF16), jax.ShapeDtypeStruct((2, size, width), F32)],
        [], 2 * (rows - 2 * rim) * width * (slots * block + 2 * size), "inner_rows",
    )


def rim_rows(basis, halos, own_ops, share, rest, tables, ids, lefts, index, size, begun):
    rows, width = basis.shape
    blocks, slots, half, block = own_ops.shape
    part, rim = blocks // 2, REACH * block
    tile = min(1024, width)

    def kernel(nb_ref, mask_ref, sec_ref, col_ref, row_ref, index_ref, up_ref, down_ref, split_ref, swapped_ref,
               head_ref, tail0_ref, tail1_ref, own_ref, share_ref, rest_ref, m0, o0, m1, o1, begun_ref,
               out_ref, unit0_ref, unit1_ref, ext):
        mine, lower = sec_ref[0] == col_ref[0], sec_ref[0] == 0
        split, swapped = split_ref[...], swapped_ref[...]
        pieces = (jnp.where(lower, swapped, split), up_ref[...], head_ref[...], tail0_ref[...],
                  tail1_ref[...], down_ref[...], jnp.where(lower, split, swapped))
        start = 0
        for piece in pieces:
            ext[start : start + piece.shape[0], :] = piece
            start += piece.shape[0]
        for i, b in enumerate((0, 1, blocks - 2, blocks - 1)):
            def halves(s, b=b):
                other = jnp.where(col_ref[0] == b // part, share_ref[b % part, s], rest_ref[b % part, s])
                return own_ref[b, s], other

            shift = REACH if b < REACH else 5 * REACH - blocks
            apply_block(b, shift, nb_ref, mask_ref, sec_ref[0], row_ref[0] * blocks, halves, ext,
                        out_ref, i * block)
        for u, (here, there, unit_ref) in enumerate(((m0, o0, unit0_ref), (m1, o1, unit1_ref))):
            total = begun_ref[u]
            for i, at in enumerate((0, rows - rim)):
                left = jnp.where(mine, here[at : at + rim, :], there[at : at + rim, :])
                total = total + transposed_dot(left, out_ref[i * rim : (i + 1) * rim, :])
            unit_ref[...] = total.astype(BF16)

    unit = [pl.BlockSpec((rows, size), lambda j, *s, u=u: (0, s[5][u])) for u in (0, 0, 1, 1)]
    last = rows // rim - 1
    halo_spec = pl.BlockSpec((block, tile), lambda j, *_: (0, j))
    unit_out = pl.BlockSpec((size, tile), lambda j, *_: (0, j))
    return call(
        kernel, (*tables, *ids, index), (width // tile,),
        [halo_spec] * 4
        + [pl.BlockSpec((2 * rim, tile), lambda j, *_: (0, j)),
           pl.BlockSpec((rim, tile), lambda j, *_: (last - 1, j)),
           pl.BlockSpec((rim, tile), lambda j, *_: (last, j)),
           fixed(own_ops), fixed(share), fixed(rest)]
        + unit + [pl.BlockSpec((2, size, tile), lambda j, *_: (0, 0, j))],
        (*halos, basis, basis, basis, own_ops, share, rest, *lefts, *lefts, begun),
        [pl.BlockSpec((2 * rim, tile), lambda j, *_: (0, j)), unit_out, unit_out],
        [jax.ShapeDtypeStruct((2 * rim, width), BF16)] + [jax.ShapeDtypeStruct((size, width), BF16)] * 2,
        [pltpu.VMEM((6 * rim, tile), BF16)],
        4 * rim * width * (slots * block + 2 * size), "rim_rows",
    )


def units(lefts, inner, rim_part, ids, index, first, count, size, dtype):
    rows = lefts[0].shape[0]
    width = inner.shape[1]
    rim = rim_part.shape[0] // 2

    def kernel(sec_ref, col_ref, row_ref, index_ref, here, there, inner_ref, rim_ref, *out_refs):
        left = jnp.where(sec_ref[0] == col_ref[0], here[...], there[...])
        total = (
            transposed_dot(left[rim : rows - rim], inner_ref[...])
            + transposed_dot(left[:rim], rim_ref[:rim, :])
            + transposed_dot(left[rows - rim :], rim_ref[rim:, :])
        ).astype(dtype)
        for u, out_ref in enumerate(out_refs):
            @pl.when(pl.program_id(0) == u)
            def _(out_ref=out_ref):
                out_ref[...] = total

    unit = pl.BlockSpec((rows, size), lambda u, *s: (0, s[3][first + u]))
    return call(
        kernel, (*ids, index), (count,), [unit, unit, fixed(inner), fixed(rim_part)],
        (*lefts, inner, rim_part),
        [pl.BlockSpec((size, width), lambda u, *_: (0, 0))] * count,
        [jax.ShapeDtypeStruct((size, width), dtype)] * count, [],
        2 * count * rows * size * width, "units",
    )


def per_device(basis, own_ops, neighbours, mask):
    rows, width = basis.shape
    blocks, slots, half, block = own_ops.shape
    sec, row, col = (lax.axis_index(name) for name in ("sec", "row", "col"))
    count = lax.axis_size("row")
    rim = REACH * block
    swap = [(0, 1), (1, 0)]
    up = [(i, i + 1) for i in range(count - 1)]
    down = [(i + 1, i) for i in range(count - 1)]

    part = blocks // 2
    split = lax.dynamic_slice_in_dim(basis, block + sec * (rows - 3 * block), block, 0)
    share = lax.dynamic_slice_in_dim(own_ops, col * part, part, 0)
    split, share, behind = lax.optimization_barrier((split, share, basis))
    split = lax.ppermute(
        split, ("sec", "row"), down + [(count + i, count + j) for i, j in up]
    )
    share = lax.ppermute(share, "sec", swap)
    from_before = lax.ppermute(basis[rows - block :], "row", up)
    from_after = lax.ppermute(basis[:block], "row", down)
    moved = lax.ppermute(behind, ("sec", "col"), [(0, 1), (3, 2)])
    share, split = lax.optimization_barrier((share, split))
    rest = lax.ppermute(share, "col", swap)
    swapped = lax.ppermute(split, "sec", swap)

    height = width * lax.axis_size("col") // lax.axis_size("sec") // count
    fars = count // 4
    far, pair, side = row // 4, row // 2 % 2, row % 2
    away = list(range(1, fars))
    plan = [
        (away, 1 - pair, 1 - side), ([0], 1 - pair, 1 - side), (away, pair, 1 - side), ([0], 1 - pair, side),
        (away, 1 - pair, side), ([0], pair, 1 - side), (away, pair, side), ([0], pair, side),
    ]
    where = [[((far + step) % fars * 2 + p) * 2 + s for step in steps] for steps, p, s in plan]
    lefts = (basis, moved)
    if fars == 2 and height % 128 == 0:
        size = height
        index = jnp.stack([w[0] for w in where]).astype(jnp.int32)
    else:
        size = -(-len(away) * height // 128) * 128
        index = jnp.arange(len(plan), dtype=jnp.int32)

        def gathered(left):
            columns = []
            for w in where:
                columns += [lax.dynamic_slice_in_dim(left, i * height, height, 1) for i in w]
                columns.append(jnp.zeros((rows, size - len(w) * height), left.dtype))
            return jnp.concatenate(columns, 1)

        lefts = tuple(gathered(left) for left in lefts)

    ids = tuple(x.astype(jnp.int32)[None] for x in (sec, col, row))
    tables = (neighbours, mask)
    inner, begun = inner_rows(basis, own_ops, share, rest, tables, ids, lefts, index, size)
    from_before, from_after, swapped, begun = lax.optimization_barrier((from_before, from_after, swapped, begun))
    rim_part, far_a, near_a = rim_rows(
        basis, (from_before, from_after, split, swapped), own_ops, share, rest, tables, ids, lefts, index,
        size, begun,
    )
    swap_side = [(i, i ^ 1) for i in range(count)]
    swap_pair = [(i, i ^ 2) for i in range(count)]

    def take(unit, i):
        return unit[: len(plan[i][0]) * height]

    def add(first, *others):
        for other in others:
            first = first + other.astype(F32)
        return first

    def after(value, *earlier):
        return lax.optimization_barrier((value, *earlier))[0]

    far_a = lax.ppermute(take(far_a, 0), "row", swap_side)
    near_a = lax.ppermute(take(near_a, 1), "row", swap_pair)
    far_b, near_b = units(lefts, inner, rim_part, ids, index, 2, 2, size, BF16)
    third = units(lefts, inner, after(rim_part, far_b), ids, index, 4, 4, size, F32)
    far_b = lax.ppermute(take(far_b, 2), "row", swap_side)
    far_c = add(take(third[0], 4), far_a).astype(BF16)
    near_c = add(take(third[1], 5), after(near_a, far_c)).astype(BF16)
    near_b = lax.ppermute(after(take(near_b, 3), near_c), "row", swap_pair)
    far_c = lax.ppermute(far_c, "row", swap_pair)
    near_c = lax.ppermute(near_c, "row", swap_side)
    far_d = add(take(third[2], 6), far_b, far_c).astype(BF16)
    parts = []
    for i, step in enumerate(away):
        route = [(g, (g + 4 * step) % count) for g in range(count)]
        parts.append(lax.ppermute(far_d[i * height : (i + 1) * height], "row", route))
    total = add(take(third[3], 7), near_b, near_c, *parts)
    return total * (1.0 / math.sqrt(rows * count))


def solution(mesh):
    return jax.shard_map(
        per_device,
        mesh=mesh,
        in_specs=(P("row", "col"), P("row", None, "sec", None), P("row", None), P("row", None)),
        out_specs=P(("sec", "row"), "col"),
        check_vma=False,
    )
```

```python
import math

import jax
import jax.numpy as jnp
from jax import lax
from jax.experimental import pallas as pl
from jax.experimental.pallas import tpu as pltpu
from jax.sharding import PartitionSpec as P

REACH = 2
VMEM_LIMIT = 32 * 1024 * 1024
F32, BF16 = jnp.float32, jnp.bfloat16


def call(kernel, scalars, grid, in_specs, operands, out_specs, out_shape, scratch, name):
    return pl.pallas_call(
        kernel,
        grid_spec=pltpu.PrefetchScalarGridSpec(
            num_scalar_prefetch=len(scalars), grid=grid, in_specs=in_specs,
            out_specs=out_specs, scratch_shapes=scratch,
        ),
        out_shape=out_shape,
        compiler_params=pltpu.CompilerParams(vmem_limit_bytes=VMEM_LIMIT),
        cost_estimate=pl.CostEstimate(flops=1, bytes_accessed=1, transcendentals=0),
        name=name,
    )(*scalars, *operands)


def fixed(array):
    return pl.BlockSpec(array.shape, lambda j, *_: (0,) * array.ndim)


def transposed_dot(left, right):
    return lax.dot_general(left, right, (((0,), (0,)), ((), ())), preferred_element_type=F32)


def masked(b, mask_ref, halves, slots):
    rows = []
    for i in range(2):
        parts = [halves(s)[i] * mask_ref[b, s].astype(F32).astype(BF16) for s in range(slots)]
        rows.append(jnp.concatenate(parts, axis=1))
    return rows


def gathered_rows(b, shift, nb_ref, first, rows_ref, block):
    return jnp.concatenate(
        [
            rows_ref[pl.ds(pl.multiple_of((nb_ref[b, s] - first + shift) * block, block), block), :]
            for s in range(nb_ref.shape[1])
        ],
        axis=0,
    )


def inner_rows(basis, own_ops, share, rest, tables, ids, lefts, index, size):
    rows, width = basis.shape
    blocks, slots, half, block = own_ops.shape
    part, rim, tile = blocks // 2, REACH * block, width // 2

    def kernel(nb_ref, mask_ref, sec_ref, col_ref, row_ref, index_ref, rows_ref, own_ref, *refs):
        shares, rests, (m0, o0, m1, o1, out_ref, unit_ref, ops_ref) = refs[:2], refs[2:4], refs[4:]
        split = shares[0].shape[0]
        mine, sec = sec_ref[0] == col_ref[0], sec_ref[0]

        def operator(b):
            def halves(s):
                piece, at = (0, b % part) if b % part < split else (1, b % part - split)
                other = jnp.where(col_ref[0] == b // part, shares[piece][at, s], rests[piece][at, s])
                return own_ref[b, s], other

            return masked(b, mask_ref, halves, slots)

        @pl.when(pl.program_id(0) == 0)
        def _():
            for i, b in enumerate((0, 1, blocks - 2, blocks - 1)):
                own, other = operator(b)
                ops_ref[i, pl.ds(pl.multiple_of(sec * half, half), half), :] = own
                ops_ref[i, pl.ds(pl.multiple_of((1 - sec) * half, half), half), :] = other

        for b in range(REACH, blocks - REACH):
            total = jnp.dot(
                jnp.concatenate(operator(b), axis=0),
                gathered_rows(b, 0, nb_ref, row_ref[0] * blocks, rows_ref, block),
                preferred_element_type=F32,
            ).astype(BF16)
            for i, place in enumerate((sec, 1 - sec)):
                start = pl.multiple_of((b - REACH) * block + place * half, half)
                out_ref[0, pl.ds(start, half), :] = total[i * half : (i + 1) * half]
        for u, (here, there) in enumerate(((m0, o0), (m1, o1))):
            left = jnp.where(mine, here[rim : rows - rim, :], there[rim : rows - rim, :])
            unit_ref[0, u] = transposed_dot(left, out_ref[0])

    unit = [pl.BlockSpec((rows, size), lambda j, *s, u=u: (0, s[5][u])) for u in (0, 0, 1, 1)]
    ops = jax.ShapeDtypeStruct((2 * REACH, block, slots * block), BF16)
    inner = rows - 2 * rim
    return call(
        kernel, (*tables, *ids, index), (2,),
        [pl.BlockSpec((rows, tile), lambda j, *_: (0, j)), fixed(own_ops), *map(fixed, (*share, *rest))] + unit,
        (basis, own_ops, *share, *rest, *lefts, *lefts),
        [pl.BlockSpec((1, inner, tile), lambda j, *_: (j, 0, 0)),
         pl.BlockSpec((1, 2, size, tile), lambda j, *_: (j, 0, 0, 0)), fixed(ops)],
        [jax.ShapeDtypeStruct((2, inner, tile), BF16), jax.ShapeDtypeStruct((2, 2, size, tile), F32), ops],
        [], "inner_rows",
    )


def rim_rows(part, basis, halos, ops, tables, ids, lefts, index, size, begun):
    rows, width = basis.shape
    block = halos[0].shape[0]
    rim = REACH * block
    blocks = rows // block
    steps = 2
    tile = width // 2 // steps

    def kernel(nb_ref, mask_ref, sec_ref, col_ref, row_ref, index_ref, up_ref, down_ref, split_ref, swapped_ref,
               head_ref, tail0_ref, tail1_ref, ops_ref, *refs):
        left_refs, (begun_ref, out_ref, *unit_refs, ext) = refs[:8], refs[8:]
        mine, lower = sec_ref[0] == col_ref[0], sec_ref[0] == 0
        split, swapped = split_ref[...], swapped_ref[...]
        ext[:block, :] = jnp.where(lower, swapped, split)
        ext[block:rim, :] = up_ref[...]
        ext[rim : 3 * rim, :] = head_ref[...]
        ext[3 * rim : 4 * rim, :] = tail0_ref[...]
        ext[4 * rim : 5 * rim, :] = tail1_ref[...]
        ext[5 * rim : 5 * rim + block, :] = down_ref[...]
        ext[5 * rim + block :, :] = jnp.where(lower, split, swapped)
        for i, b in enumerate((0, 1, blocks - 2, blocks - 1)):
            shift = REACH if b < REACH else 5 * REACH - blocks
            out_ref[i * block : (i + 1) * block, :] = jnp.dot(
                ops_ref[i],
                gathered_rows(b, shift, nb_ref, row_ref[0] * blocks, ext, block),
                preferred_element_type=F32,
            ).astype(BF16)
        for u, unit_ref in enumerate(unit_refs):
            total = begun_ref[0, u]
            for i in range(2):
                here, there = left_refs[4 * u + 2 * i : 4 * u + 2 * i + 2]
                left = jnp.where(mine, here[...], there[...])
                total = total + transposed_dot(left, out_ref[i * rim : (i + 1) * rim, :])
            unit_ref[...] = total.astype(BF16)

    last = rows // rim - 1
    unit = [
        pl.BlockSpec((rim, size), lambda j, *s, u=u, at=at: (at, s[5][u]))
        for u in range(2) for at in (0, last) for _ in range(2)
    ]

    def across(height, at=0):
        return pl.BlockSpec((height, tile), lambda j, *_: (at, part * steps + j))

    def out(height):
        return pl.BlockSpec((height, tile), lambda j, *_: (0, j))

    return call(
        kernel, (*tables, *ids, index), (steps,),
        [across(block)] * 4 + [across(2 * rim), across(rim, last - 1), across(rim, last), fixed(ops)]
        + unit + [pl.BlockSpec((1, 2, size, tile), lambda j, *_: (part, 0, 0, j))],
        (*halos, basis, basis, basis, ops, *(lefts * 4), begun),
        [out(2 * rim), out(size), out(size)],
        [jax.ShapeDtypeStruct((2 * rim, width // 2), BF16)]
        + [jax.ShapeDtypeStruct((size, width // 2), BF16)] * 2,
        [pltpu.VMEM((6 * rim, tile), BF16)], "rim_rows",
    )


def units(part, which, lefts, inner, rim_part, ids, index, size, dtype):
    rows = lefts[0].shape[0]
    width = inner.shape[2]
    rim = rim_part.shape[0] // 2
    first, count = which[0], len(which)
    assert list(which) == list(range(first, first + count))

    def kernel(sec_ref, col_ref, row_ref, index_ref, here, there, inner_ref, rim_ref, *out_refs):
        left = jnp.where(sec_ref[0] == col_ref[0], here[...], there[...])
        total = (
            transposed_dot(left[rim : rows - rim], inner_ref[0])
            + transposed_dot(left[:rim], rim_ref[:rim, :])
            + transposed_dot(left[rows - rim :], rim_ref[rim:, :])
        ).astype(dtype)
        for u, out_ref in enumerate(out_refs):
            @pl.when(pl.program_id(0) == u)
            def _(out_ref=out_ref):
                out_ref[...] = total

    unit = pl.BlockSpec((rows, size), lambda u, *s: (0, s[3][first + u]))
    return call(
        kernel, (*ids, index), (count,),
        [unit, unit, pl.BlockSpec((1, *inner.shape[1:]), lambda u, *_: (part, 0, 0)), fixed(rim_part)],
        (*lefts, inner, rim_part),
        [pl.BlockSpec((size, width), lambda u, *_: (0, 0))] * count,
        [jax.ShapeDtypeStruct((size, width), dtype)] * count, [], "units",
    )


def finish(halves, scale):
    height, width = halves[0][0].shape
    count = len(halves[0])

    def kernel(*refs):
        for part, chosen in enumerate((refs[:count], refs[count:-1])):
            @pl.when(pl.program_id(0) == part)
            def _(chosen=chosen):
                total = chosen[0][...]
                for ref in chosen[1:]:
                    total = total + ref[...].astype(F32)
                refs[-1][...] = total * scale

    operands = [x for half in halves for x in half]
    return call(
        kernel, (), (2,), [fixed(x) for x in operands], operands,
        pl.BlockSpec((height, width), lambda j: (0, j)),
        jax.ShapeDtypeStruct((height, 2 * width), F32), [], "finish",
    )


def per_device(basis, own_ops, neighbours, mask):
    rows, width = basis.shape
    blocks, slots, half, block = own_ops.shape
    sec, row, col = (lax.axis_index(name) for name in ("sec", "row", "col"))
    count = lax.axis_size("row")
    rim = REACH * block
    swap = [(0, 1), (1, 0)]
    up = [(i, (i + 1) % count) for i in range(count)]
    down = [(j, i) for i, j in up]

    def after(value, *earlier):
        return lax.optimization_barrier((value, earlier))[0]

    split = lax.dynamic_slice_in_dim(basis, block + sec * (rows - 3 * block), block, 0)
    behind = after(basis, split)
    split = lax.ppermute(split, ("sec", "row"), down + [(count + i, count + j) for i, j in up])
    part = blocks // 2
    cuts = (0, part // 2, part)
    share = [
        lax.dynamic_slice_in_dim(own_ops, col * part + i, j - i, 0) for i, j in zip(cuts, cuts[1:])
    ]
    behind = after(behind, share)
    share = [lax.ppermute(x, "sec", swap) for x in share]
    from_before = lax.ppermute(behind[rows - block :], "row", up)
    from_after = lax.ppermute(behind[:block], "row", down)
    moved = lax.ppermute(behind, "col", swap)
    rest = [lax.ppermute(x, "col", swap) for x in share]
    swapped = lax.ppermute(split, "sec", swap)

    height = width * lax.axis_size("col") // lax.axis_size("sec") // count
    fars = count // 4
    far, pair, side = row // 4, row // 2 % 2, row % 2
    away = list(range(1, fars))
    plan = [
        (away, 1 - pair, 1 - side), ([0], 1 - pair, 1 - side), (away, pair, 1 - side), ([0], 1 - pair, side),
        (away, 1 - pair, side), ([0], pair, 1 - side), (away, pair, side), ([0], pair, side),
    ]
    where = [[((far + step) % fars * 2 + p) * 2 + s for step in steps] for steps, p, s in plan]
    lefts = (basis, moved)
    if fars == 2 and height % 128 == 0:
        size = height
        index = jnp.stack([w[0] for w in where]).astype(jnp.int32)
    else:
        size = -(-len(away) * height // 128) * 128
        index = jnp.arange(len(plan), dtype=jnp.int32)

        def gathered(left):
            columns = []
            for w in where:
                columns += [lax.dynamic_slice_in_dim(left, i * height, height, 1) for i in w]
                columns.append(jnp.zeros((rows, size - len(w) * height), left.dtype))
            return jnp.concatenate(columns, 1)

        lefts = tuple(gathered(left) for left in lefts)

    ids = tuple(x.astype(jnp.int32)[None] for x in (sec, col, row))
    tables = (neighbours, mask)
    inner, begun, ops = inner_rows(basis, own_ops, share, rest, tables, ids, lefts, index, size)
    halos = (from_before, from_after, split, swapped)
    swap_side = [(i, i ^ 1) for i in range(count)]
    swap_pair = [(i, i ^ 2) for i in range(count)]

    def rim_half(part, halos):
        rim_part, a, b = rim_rows(part, basis, halos, ops, tables, ids, lefts, index, size, begun)
        return rim_part, a[: len(away) * height], b[:height]

    def unit_half(part, which, rim_part, dtype):
        made = units(part, which, lefts, inner, rim_part, ids, index, size, dtype)
        return [x[: len(plan[i][0]) * height] for i, x in zip(which, made)]

    def to_side(x):
        return lax.ppermute(x, "row", swap_side)

    def to_pair(x):
        return lax.ppermute(x, "row", swap_pair)

    def to_far(x):
        parts = []
        for i, step in enumerate(away):
            route = [(g, (g + 4 * step) % count) for g in range(count)]
            parts.append(lax.ppermute(x[i * height : (i + 1) * height], "row", route))
        return parts

    def add32(first, *others):
        for other in others:
            first = first + other.astype(F32)
        return first

    def add(first, *others):
        return add32(first, *others).astype(BF16)

    rim0, far_a0, near_a0 = rim_half(0, halos)
    far_a0, near_a0 = to_side(far_a0), to_pair(near_a0)
    far_b0, near_b0 = unit_half(0, (2, 3), rim0, BF16)
    far_b0 = to_side(far_b0)
    rim1, far_a1, near_a1 = rim_half(1, (after(halos[0], near_b0), *halos[1:]))
    far_a1 = to_side(far_a1)
    far_c0, near_c0, far_d0, own0 = unit_half(0, (4, 5, 6, 7), after(rim0, rim1), F32)
    far_c0 = add(far_c0, far_a0)
    near_c0 = add(near_c0, after(near_a0, far_c0))
    far_c0 = to_pair(far_c0)
    near_b0 = to_pair(after(near_b0, near_c0))
    late1 = after(rim1, near_c0)
    (far_b1,) = unit_half(1, (2,), late1, BF16)
    near_b1, far_c1, near_c1, far_d1, own1 = unit_half(1, (3, 4, 5, 6, 7), after(late1, far_b1), F32)
    far_b1 = to_side(far_b1)
    near_a1 = to_side(after(near_a1, far_c1))
    far_d0 = add(far_d0, after(far_b0, far_c1), far_c0)
    far_c1 = add(far_c1, after(far_a1, far_d0))
    far_d0 = to_far(far_d0)
    own0 = add32(own0, after(near_b0, far_c1), *far_d0)
    near_c0, near_c1 = after((near_c0, near_c1), far_c1)
    far_c1 = to_pair(far_c1)
    far_d1 = add(far_d1, after(far_b1, own0), far_c1)
    near_b1 = add(near_b1, after(near_a1, far_d1))
    far_d1 = to_far(far_d1)
    own1 = add32(own1, *after(far_d1, near_b1))
    near_b1 = to_pair(near_b1)
    near_c0 = to_side(near_c0)
    near_c1 = to_side(near_c1.astype(BF16))
    near_b1, near_c0, near_c1 = after((near_b1, near_c0, near_c1), own1)
    return finish(
        ((own0, near_c0), (own1, near_b1, near_c1)), 1.0 / math.sqrt(rows * count)
    )


def solution(mesh):
    return jax.shard_map(
        per_device,
        mesh=mesh,
        in_specs=(P("row", "col"), P("row", None, "sec", None), P("row", None), P("row", None)),
        out_specs=P(("sec", "row"), "col"),
        check_vma=False,
    )
```

```python
import math

import jax
import jax.numpy as jnp
from jax import lax
from jax.experimental import pallas as pl
from jax.experimental.pallas import tpu as pltpu
from jax.sharding import PartitionSpec as P

REACH = 2
VMEM_LIMIT = 32 * 1024 * 1024
F32, BF16 = jnp.float32, jnp.bfloat16


def call(kernel, scalars, grid, in_specs, operands, out_specs, out_shape, scratch, name):
    return pl.pallas_call(
        kernel,
        grid_spec=pltpu.PrefetchScalarGridSpec(
            num_scalar_prefetch=len(scalars), grid=grid, in_specs=in_specs,
            out_specs=out_specs, scratch_shapes=scratch,
        ),
        out_shape=out_shape,
        compiler_params=pltpu.CompilerParams(vmem_limit_bytes=VMEM_LIMIT),
        cost_estimate=pl.CostEstimate(flops=1, bytes_accessed=1, transcendentals=0),
        name=name,
    )(*scalars, *operands)


def fixed(array):
    return pl.BlockSpec(array.shape, lambda j, *_: (0,) * array.ndim)


def transposed_dot(left, right):
    return lax.dot_general(left, right, (((0,), (0,)), ((), ())), preferred_element_type=F32)


def masked(b, mask_ref, halves, slots):
    rows = []
    for i in range(2):
        parts = [halves(s)[i] * mask_ref[b, s].astype(F32).astype(BF16) for s in range(slots)]
        rows.append(jnp.concatenate(parts, axis=1))
    return rows


def gathered_rows(b, shift, nb_ref, first, rows_ref, block):
    return jnp.concatenate(
        [
            rows_ref[pl.ds(pl.multiple_of((nb_ref[b, s] - first + shift) * block, block), block), :]
            for s in range(nb_ref.shape[1])
        ],
        axis=0,
    )


def inner_rows(basis, own_ops, share, rest, tables, ids, lefts, index, size):
    rows, width = basis.shape
    blocks, slots, half, block = own_ops.shape
    part, rim, tile = blocks // 2, REACH * block, width // 2

    def kernel(nb_ref, mask_ref, sec_ref, col_ref, row_ref, index_ref, rows_ref, own_ref, *refs):
        shares, rests, (m0, o0, m1, o1, out_ref, unit_ref, ops_ref) = refs[:2], refs[2:4], refs[4:]
        split = shares[0].shape[0]
        mine, sec = sec_ref[0] == col_ref[0], sec_ref[0]

        def operator(b):
            def halves(s):
                piece, at = (0, b % part) if b % part < split else (1, b % part - split)
                other = jnp.where(col_ref[0] == b // part, shares[piece][at, s], rests[piece][at, s])
                return own_ref[b, s], other

            return masked(b, mask_ref, halves, slots)

        @pl.when(pl.program_id(0) == 0)
        def _():
            for i, b in enumerate((0, 1, blocks - 2, blocks - 1)):
                own, other = operator(b)
                ops_ref[i, pl.ds(pl.multiple_of(sec * half, half), half), :] = own
                ops_ref[i, pl.ds(pl.multiple_of((1 - sec) * half, half), half), :] = other

        for b in range(REACH, blocks - REACH):
            total = jnp.dot(
                jnp.concatenate(operator(b), axis=0),
                gathered_rows(b, 0, nb_ref, row_ref[0] * blocks, rows_ref, block),
                preferred_element_type=F32,
            ).astype(BF16)
            for i, place in enumerate((sec, 1 - sec)):
                start = pl.multiple_of((b - REACH) * block + place * half, half)
                out_ref[0, pl.ds(start, half), :] = total[i * half : (i + 1) * half]
        for u, (here, there) in enumerate(((m0, o0), (m1, o1))):
            left = jnp.where(mine, here[rim : rows - rim, :], there[rim : rows - rim, :])
            unit_ref[0, u] = transposed_dot(left, out_ref[0])

    unit = [pl.BlockSpec((rows, size), lambda j, *s, u=u: (0, s[5][u])) for u in (0, 0, 1, 1)]
    ops = jax.ShapeDtypeStruct((2 * REACH, block, slots * block), BF16)
    inner = rows - 2 * rim
    return call(
        kernel, (*tables, *ids, index), (2,),
        [pl.BlockSpec((rows, tile), lambda j, *_: (0, j)), fixed(own_ops), *map(fixed, (*share, *rest))] + unit,
        (basis, own_ops, *share, *rest, *lefts, *lefts),
        [pl.BlockSpec((1, inner, tile), lambda j, *_: (j, 0, 0)),
         pl.BlockSpec((1, 2, size, tile), lambda j, *_: (j, 0, 0, 0)), fixed(ops)],
        [jax.ShapeDtypeStruct((2, inner, tile), BF16), jax.ShapeDtypeStruct((2, 2, size, tile), F32), ops],
        [], "inner_rows",
    )


def rim_rows(part, basis, halos, ops, tables, ids, lefts, index, size, begun):
    rows, width = basis.shape
    block = halos[0].shape[0]
    rim = REACH * block
    blocks = rows // block
    steps = 2
    tile = width // 2 // steps

    def kernel(nb_ref, mask_ref, sec_ref, col_ref, row_ref, index_ref, up_ref, down_ref, split_ref, swapped_ref,
               head_ref, tail0_ref, tail1_ref, ops_ref, *refs):
        left_refs, (begun_ref, out_ref, *unit_refs, ext) = refs[:8], refs[8:]
        mine, lower = sec_ref[0] == col_ref[0], sec_ref[0] == 0
        split, swapped = split_ref[...], swapped_ref[...]
        ext[:block, :] = jnp.where(lower, swapped, split)
        ext[block:rim, :] = up_ref[...]
        ext[rim : 3 * rim, :] = head_ref[...]
        ext[3 * rim : 4 * rim, :] = tail0_ref[...]
        ext[4 * rim : 5 * rim, :] = tail1_ref[...]
        ext[5 * rim : 5 * rim + block, :] = down_ref[...]
        ext[5 * rim + block :, :] = jnp.where(lower, split, swapped)
        for i, b in enumerate((0, 1, blocks - 2, blocks - 1)):
            shift = REACH if b < REACH else 5 * REACH - blocks
            out_ref[i * block : (i + 1) * block, :] = jnp.dot(
                ops_ref[i],
                gathered_rows(b, shift, nb_ref, row_ref[0] * blocks, ext, block),
                preferred_element_type=F32,
            ).astype(BF16)
        for u, unit_ref in enumerate(unit_refs):
            total = begun_ref[0, u]
            for i in range(2):
                here, there = left_refs[4 * u + 2 * i : 4 * u + 2 * i + 2]
                left = jnp.where(mine, here[...], there[...])
                total = total + transposed_dot(left, out_ref[i * rim : (i + 1) * rim, :])
            unit_ref[...] = total.astype(BF16)

    last = rows // rim - 1
    unit = [
        pl.BlockSpec((rim, size), lambda j, *s, u=u, at=at: (at, s[5][u]))
        for u in range(2) for at in (0, last) for _ in range(2)
    ]

    def across(height, at=0):
        return pl.BlockSpec((height, tile), lambda j, *_: (at, part * steps + j))

    def out(height):
        return pl.BlockSpec((height, tile), lambda j, *_: (0, j))

    return call(
        kernel, (*tables, *ids, index), (steps,),
        [across(block)] * 4 + [across(2 * rim), across(rim, last - 1), across(rim, last), fixed(ops)]
        + unit + [pl.BlockSpec((1, 2, size, tile), lambda j, *_: (part, 0, 0, j))],
        (*halos, basis, basis, basis, ops, *(lefts * 4), begun),
        [out(2 * rim), out(size), out(size)],
        [jax.ShapeDtypeStruct((2 * rim, width // 2), BF16)]
        + [jax.ShapeDtypeStruct((size, width // 2), BF16)] * 2,
        [pltpu.VMEM((6 * rim, tile), BF16)], "rim_rows",
    )


def units(part, which, lefts, inner, rim_part, ids, index, size, dtypes):
    rows = lefts[0].shape[0]
    width = inner.shape[2]
    rim = rim_part.shape[0] // 2
    first, count = which[0], len(which)
    assert list(which) == list(range(first, first + count))

    def kernel(sec_ref, col_ref, row_ref, index_ref, here, there, inner_ref, rim_ref, *out_refs):
        left = jnp.where(sec_ref[0] == col_ref[0], here[...], there[...])
        total = (
            transposed_dot(left[rim : rows - rim], inner_ref[0])
            + transposed_dot(left[:rim], rim_ref[:rim, :])
            + transposed_dot(left[rows - rim :], rim_ref[rim:, :])
        )
        for u, out_ref in enumerate(out_refs):
            @pl.when(pl.program_id(0) == u)
            def _(out_ref=out_ref):
                out_ref[...] = total.astype(out_ref.dtype)

    unit = pl.BlockSpec((rows, size), lambda u, *s: (0, s[3][first + u]))
    return call(
        kernel, (*ids, index), (count,),
        [unit, unit, pl.BlockSpec((1, *inner.shape[1:]), lambda u, *_: (part, 0, 0)), fixed(rim_part)],
        (*lefts, inner, rim_part),
        [pl.BlockSpec((size, width), lambda u, *_: (0, 0))] * count,
        [jax.ShapeDtypeStruct((size, width), dtype) for dtype in dtypes], [], "units",
    )


def finish(halves, scale):
    height, width = halves[0][0].shape
    count = len(halves[0])

    def kernel(*refs):
        for part, chosen in enumerate((refs[:count], refs[count:-1])):
            @pl.when(pl.program_id(0) == part)
            def _(chosen=chosen):
                total = chosen[0][...]
                for ref in chosen[1:]:
                    total = total + ref[...].astype(F32)
                refs[-1][...] = total * scale

    operands = [x for half in halves for x in half]
    return call(
        kernel, (), (2,), [fixed(x) for x in operands], operands,
        pl.BlockSpec((height, width), lambda j: (0, j)),
        jax.ShapeDtypeStruct((height, 2 * width), F32), [], "finish",
    )


def per_device(basis, own_ops, neighbours, mask):
    rows, width = basis.shape
    blocks, slots, half, block = own_ops.shape
    sec, row, col = (lax.axis_index(name) for name in ("sec", "row", "col"))
    count = lax.axis_size("row")
    rim = REACH * block
    swap = [(0, 1), (1, 0)]
    up = [(i, (i + 1) % count) for i in range(count)]
    down = [(j, i) for i, j in up]

    def after(value, *earlier):
        return lax.optimization_barrier((value, earlier))[0]

    split = lax.dynamic_slice_in_dim(basis, block + sec * (rows - 3 * block), block, 0)
    behind = after(basis, split)
    split = lax.ppermute(split, ("sec", "row"), down + [(count + i, count + j) for i, j in up])
    part = blocks // 2
    cuts = (0, part // 2, part)
    share = [
        lax.dynamic_slice_in_dim(own_ops, col * part + i, j - i, 0) for i, j in zip(cuts, cuts[1:])
    ]
    behind = after(behind, share)
    share = [lax.ppermute(x, "sec", swap) for x in share]
    from_before = lax.ppermute(behind[rows - block :], "row", up)
    from_after = lax.ppermute(behind[:block], "row", down)
    moved = lax.ppermute(behind, "col", swap)
    rest = [lax.ppermute(x, "col", swap) for x in share]
    swapped = lax.ppermute(split, "sec", swap)

    height = width * lax.axis_size("col") // lax.axis_size("sec") // count
    fars = count // 4
    far, pair, side = row // 4, row // 2 % 2, row % 2
    away = list(range(1, fars))
    plan = [
        (away, 1 - pair, 1 - side), ([0], 1 - pair, 1 - side), (away, pair, 1 - side), ([0], 1 - pair, side),
        (away, 1 - pair, side), ([0], pair, 1 - side), (away, pair, side), ([0], pair, side),
    ]
    where = [[((far + step) % fars * 2 + p) * 2 + s for step in steps] for steps, p, s in plan]
    lefts = (basis, moved)
    if fars == 2 and height % 128 == 0:
        size = height
        index = jnp.stack([w[0] for w in where]).astype(jnp.int32)
    else:
        size = -(-len(away) * height // 128) * 128
        index = jnp.arange(len(plan), dtype=jnp.int32)

        def gathered(left):
            columns = []
            for w in where:
                columns += [lax.dynamic_slice_in_dim(left, i * height, height, 1) for i in w]
                columns.append(jnp.zeros((rows, size - len(w) * height), left.dtype))
            return jnp.concatenate(columns, 1)

        lefts = tuple(gathered(left) for left in lefts)

    ids = tuple(x.astype(jnp.int32)[None] for x in (sec, col, row))
    tables = (neighbours, mask)
    inner, begun, ops = inner_rows(basis, own_ops, share, rest, tables, ids, lefts, index, size)
    halos = (from_before, from_after, split, swapped)
    swap_side = [(i, i ^ 1) for i in range(count)]
    swap_pair = [(i, i ^ 2) for i in range(count)]

    def rim_half(part, halos):
        rim_part, a, b = rim_rows(part, basis, halos, ops, tables, ids, lefts, index, size, begun)
        return rim_part, a[: len(away) * height], b[:height]

    def unit_half(part, which, rim_part, *dtypes):
        made = units(part, which, lefts, inner, rim_part, ids, index, size, dtypes)
        return [x[: len(plan[i][0]) * height] for i, x in zip(which, made)]

    def to_side(x):
        return lax.ppermute(x, "row", swap_side)

    def to_pair(x):
        return lax.ppermute(x, "row", swap_pair)

    def to_far(x):
        parts = []
        for i, step in enumerate(away):
            route = [(g, (g + 4 * step) % count) for g in range(count)]
            parts.append(lax.ppermute(x[i * height : (i + 1) * height], "row", route))
        return parts

    def add32(first, *others):
        for other in others:
            first = first + other.astype(F32)
        return first

    def add(first, *others):
        return add32(first, *others).astype(BF16)

    rim0, far_a0, near_a0 = rim_half(0, halos)
    far_a0, near_a0 = to_side(far_a0), to_pair(near_a0)
    far_b0, near_b0, far_c0 = unit_half(0, (2, 3, 4), rim0, BF16, BF16, F32)
    rim1, far_a1, near_a1 = rim_half(1, (after(halos[0], far_c0), *halos[1:]))
    far_b0 = to_side(far_b0)
    far_c0 = add(far_c0, after(far_a0, rim1))
    near_c0, far_d0, own0 = unit_half(0, (5, 6, 7), after(rim0, far_c0), F32, F32, F32)
    far_c0_sum = far_c0
    far_c0 = to_pair(far_c0)
    far_a1 = to_side(far_a1)
    near_c0 = add(near_c0, after(near_a0, own0))
    far_b1, near_b1, far_c1 = unit_half(1, (2, 3, 4), after(rim1, near_c0), BF16, F32, F32)
    far_b1 = to_side(far_b1)
    far_d0 = add(far_d0, after(far_b0, far_c1), far_c0)
    near_b0 = to_pair(after(near_b0, far_c0_sum))
    near_a1 = to_side(after(near_a1, far_d0))
    own0 = add32(own0, after(near_b0, far_d0))
    far_c1 = add(far_c1, after(far_a1, own0))
    far_d0 = to_far(far_d0)
    near_c1, far_d1, own1 = unit_half(1, (5, 6, 7), after(rim1, far_c1), BF16, F32, F32)
    far_c1 = to_pair(far_c1)
    near_b1 = add(near_b1, after(near_a1, far_d1))
    near_c0, near_c1 = after((near_c0, near_c1), near_b1)
    own0 = add32(own0, *after(far_d0, near_b1))
    near_b1 = to_pair(near_b1)
    far_d1 = add(far_d1, after(far_b1, own0), far_c1)
    near_c0 = to_side(near_c0)
    own0 = add32(own0, after(near_c0, far_d1))
    far_d1 = to_far(far_d1)
    own1 = add32(own1, *after(far_d1, own0))
    near_c1 = to_side(near_c1)
    near_b1, near_c1 = after((near_b1, near_c1), own1)
    return finish(((own0,), (own1, near_b1, near_c1)), 1.0 / math.sqrt(rows * count))


def solution(mesh):
    return jax.shard_map(
        per_device,
        mesh=mesh,
        in_specs=(P("row", "col"), P("row", None, "sec", None), P("row", None), P("row", None)),
        out_specs=P(("sec", "row"), "col"),
        check_vma=False,
    )
```

```python
import math

import jax
import jax.numpy as jnp
from jax import lax
from jax.experimental import pallas as pl
from jax.experimental.pallas import tpu as pltpu
from jax.sharding import PartitionSpec as P

REACH = 2
VMEM_LIMIT = 32 * 1024 * 1024
F32, BF16 = jnp.float32, jnp.bfloat16


def call(kernel, scalars, grid, in_specs, operands, out_specs, out_shape, scratch, name):
    return pl.pallas_call(
        kernel,
        grid_spec=pltpu.PrefetchScalarGridSpec(
            num_scalar_prefetch=len(scalars), grid=grid, in_specs=in_specs,
            out_specs=out_specs, scratch_shapes=scratch,
        ),
        out_shape=out_shape,
        compiler_params=pltpu.CompilerParams(vmem_limit_bytes=VMEM_LIMIT),
        cost_estimate=pl.CostEstimate(flops=1, bytes_accessed=1, transcendentals=0),
        name=name,
    )(*scalars, *operands)


def fixed(array):
    return pl.BlockSpec(array.shape, lambda j, *_: (0,) * array.ndim)


def transposed_dot(left, right):
    return lax.dot_general(left, right, (((0,), (0,)), ((), ())), preferred_element_type=F32)


def masked(b, mask_ref, halves, slots):
    rows = []
    for i in range(2):
        parts = [halves(s)[i] * mask_ref[b, s].astype(F32).astype(BF16) for s in range(slots)]
        rows.append(jnp.concatenate(parts, axis=1))
    return rows


def gathered_rows(b, shift, nb_ref, first, rows_ref, block):
    return jnp.concatenate(
        [
            rows_ref[pl.ds(pl.multiple_of((nb_ref[b, s] - first + shift) * block, block), block), :]
            for s in range(nb_ref.shape[1])
        ],
        axis=0,
    )


def inner_rows(basis, own_ops, share, rest, tables, ids, lefts, index, size):
    rows, width = basis.shape
    blocks, slots, half, block = own_ops.shape
    part, rim, tile = blocks // 2, REACH * block, width // 2

    def kernel(nb_ref, mask_ref, sec_ref, col_ref, row_ref, index_ref, rows_ref, own_ref, *refs):
        shares, rests, (m0, o0, m1, o1, out_ref, unit_ref, ops_ref) = refs[:2], refs[2:4], refs[4:]
        split = shares[0].shape[0]
        mine, sec = sec_ref[0] == col_ref[0], sec_ref[0]

        def operator(b):
            def halves(s):
                piece, at = (0, b % part) if b % part < split else (1, b % part - split)
                other = jnp.where(col_ref[0] == b // part, shares[piece][at, s], rests[piece][at, s])
                return own_ref[b, s], other

            return masked(b, mask_ref, halves, slots)

        @pl.when(pl.program_id(0) == 0)
        def _():
            for i, b in enumerate((0, 1, blocks - 2, blocks - 1)):
                own, other = operator(b)
                ops_ref[i, pl.ds(pl.multiple_of(sec * half, half), half), :] = own
                ops_ref[i, pl.ds(pl.multiple_of((1 - sec) * half, half), half), :] = other

        for b in range(REACH, blocks - REACH):
            total = jnp.dot(
                jnp.concatenate(operator(b), axis=0),
                gathered_rows(b, 0, nb_ref, row_ref[0] * blocks, rows_ref, block),
                preferred_element_type=F32,
            ).astype(BF16)
            for i, place in enumerate((sec, 1 - sec)):
                start = pl.multiple_of((b - REACH) * block + place * half, half)
                out_ref[0, pl.ds(start, half), :] = total[i * half : (i + 1) * half]
        for u, (here, there) in enumerate(((m0, o0), (m1, o1))):
            left = jnp.where(mine, here[rim : rows - rim, :], there[rim : rows - rim, :])
            unit_ref[0, u] = transposed_dot(left, out_ref[0])

    unit = [pl.BlockSpec((rows, size), lambda j, *s, u=u: (0, s[5][u])) for u in (0, 0, 1, 1)]
    ops = jax.ShapeDtypeStruct((2 * REACH, block, slots * block), BF16)
    inner = rows - 2 * rim
    return call(
        kernel, (*tables, *ids, index), (2,),
        [pl.BlockSpec((rows, tile), lambda j, *_: (0, j)), fixed(own_ops), *map(fixed, (*share, *rest))] + unit,
        (basis, own_ops, *share, *rest, *lefts, *lefts),
        [pl.BlockSpec((1, inner, tile), lambda j, *_: (j, 0, 0)),
         pl.BlockSpec((1, 2, size, tile), lambda j, *_: (j, 0, 0, 0)), fixed(ops)],
        [jax.ShapeDtypeStruct((2, inner, tile), BF16), jax.ShapeDtypeStruct((2, 2, size, tile), F32), ops],
        [], "inner_rows",
    )


def rim_rows(part, basis, halos, ops, tables, ids, lefts, index, size, begun):
    rows, width = basis.shape
    block = halos[0].shape[0]
    rim = REACH * block
    blocks = rows // block
    steps = 2
    tile = width // 2 // steps

    def kernel(nb_ref, mask_ref, sec_ref, col_ref, row_ref, index_ref, up_ref, down_ref, split_ref, swapped_ref,
               head_ref, tail0_ref, tail1_ref, ops_ref, *refs):
        left_refs, (begun_ref, out_ref, *unit_refs, ext) = refs[:8], refs[8:]
        mine, lower = sec_ref[0] == col_ref[0], sec_ref[0] == 0
        split, swapped = split_ref[...], swapped_ref[...]
        ext[:block, :] = jnp.where(lower, swapped, split)
        ext[block:rim, :] = up_ref[...]
        ext[rim : 3 * rim, :] = head_ref[...]
        ext[3 * rim : 4 * rim, :] = tail0_ref[...]
        ext[4 * rim : 5 * rim, :] = tail1_ref[...]
        ext[5 * rim : 5 * rim + block, :] = down_ref[...]
        ext[5 * rim + block :, :] = jnp.where(lower, split, swapped)
        for i, b in enumerate((0, 1, blocks - 2, blocks - 1)):
            shift = REACH if b < REACH else 5 * REACH - blocks
            out_ref[i * block : (i + 1) * block, :] = jnp.dot(
                ops_ref[i],
                gathered_rows(b, shift, nb_ref, row_ref[0] * blocks, ext, block),
                preferred_element_type=F32,
            ).astype(BF16)
        for u, unit_ref in enumerate(unit_refs):
            total = begun_ref[0, u]
            for i in range(2):
                here, there = left_refs[4 * u + 2 * i : 4 * u + 2 * i + 2]
                left = jnp.where(mine, here[...], there[...])
                total = total + transposed_dot(left, out_ref[i * rim : (i + 1) * rim, :])
            unit_ref[...] = total.astype(BF16)

    last = rows // rim - 1
    unit = [
        pl.BlockSpec((rim, size), lambda j, *s, u=u, at=at: (at, s[5][u]))
        for u in range(2) for at in (0, last) for _ in range(2)
    ]

    def across(height, at=0):
        return pl.BlockSpec((height, tile), lambda j, *_: (at, part * steps + j))

    def out(height):
        return pl.BlockSpec((height, tile), lambda j, *_: (0, j))

    return call(
        kernel, (*tables, *ids, index), (steps,),
        [across(block)] * 4 + [across(2 * rim), across(rim, last - 1), across(rim, last), fixed(ops)]
        + unit + [pl.BlockSpec((1, 2, size, tile), lambda j, *_: (part, 0, 0, j))],
        (*halos, basis, basis, basis, ops, *(lefts * 4), begun),
        [out(2 * rim), out(size), out(size)],
        [jax.ShapeDtypeStruct((2 * rim, width // 2), BF16)]
        + [jax.ShapeDtypeStruct((size, width // 2), BF16)] * 2,
        [pltpu.VMEM((6 * rim, tile), BF16)], "rim_rows",
    )


def units(part, which, lefts, inner, rim_part, ids, index, size, dtypes):
    rows = lefts[0].shape[0]
    width = inner.shape[2]
    rim = rim_part.shape[0] // 2
    first, count = which[0], len(which)
    assert list(which) == list(range(first, first + count))

    def kernel(sec_ref, col_ref, row_ref, index_ref, here, there, inner_ref, rim_ref, *out_refs):
        left = jnp.where(sec_ref[0] == col_ref[0], here[...], there[...])
        total = (
            transposed_dot(left[rim : rows - rim], inner_ref[0])
            + transposed_dot(left[:rim], rim_ref[:rim, :])
            + transposed_dot(left[rows - rim :], rim_ref[rim:, :])
        )
        for u, out_ref in enumerate(out_refs):
            @pl.when(pl.program_id(0) == u)
            def _(out_ref=out_ref):
                out_ref[...] = total.astype(out_ref.dtype)

    unit = pl.BlockSpec((rows, size), lambda u, *s: (0, s[3][first + u]))
    return call(
        kernel, (*ids, index), (count,),
        [unit, unit, pl.BlockSpec((1, *inner.shape[1:]), lambda u, *_: (part, 0, 0)), fixed(rim_part)],
        (*lefts, inner, rim_part),
        [pl.BlockSpec((size, width), lambda u, *_: (0, 0))] * count,
        [jax.ShapeDtypeStruct((size, width), dtype) for dtype in dtypes], [], "units",
    )


def finish(halves, scale):
    height, width = halves[0][0].shape
    count = len(halves[0])

    def kernel(*refs):
        for part, chosen in enumerate((refs[:count], refs[count:-1])):
            @pl.when(pl.program_id(0) == part)
            def _(chosen=chosen):
                total = chosen[0][...]
                for ref in chosen[1:]:
                    total = total + ref[...].astype(F32)
                refs[-1][...] = total * scale

    operands = [x for half in halves for x in half]
    return call(
        kernel, (), (2,), [fixed(x) for x in operands], operands,
        pl.BlockSpec((height, width), lambda j: (0, j)),
        jax.ShapeDtypeStruct((height, 2 * width), F32), [], "finish",
    )


def per_device(basis, own_ops, neighbours, mask):
    rows, width = basis.shape
    blocks, slots, half, block = own_ops.shape
    sec, row, col = (lax.axis_index(name) for name in ("sec", "row", "col"))
    count = lax.axis_size("row")
    rim = REACH * block
    swap = [(0, 1), (1, 0)]
    up = [(i, (i + 1) % count) for i in range(count)]
    down = [(j, i) for i, j in up]

    def after(value, *earlier):
        return lax.optimization_barrier((value, earlier))[0]

    split = lax.dynamic_slice_in_dim(basis, block + sec * (rows - 3 * block), block, 0)
    behind = after(basis, split)
    split = lax.ppermute(split, ("sec", "row"), down + [(count + i, count + j) for i, j in up])
    part = blocks // 2
    cuts = (0, part // 2, part)
    share = [
        lax.dynamic_slice_in_dim(own_ops, col * part + i, j - i, 0) for i, j in zip(cuts, cuts[1:])
    ]
    behind = after(behind, share)
    share = [lax.ppermute(x, "sec", swap) for x in share]
    from_before = lax.ppermute(behind[rows - block :], "row", up)
    from_after = lax.ppermute(behind[:block], "row", down)
    moved = lax.ppermute(behind, "col", swap)
    rest = [lax.ppermute(x, "col", swap) for x in share]
    swapped = lax.ppermute(split, "sec", swap)

    height = width * lax.axis_size("col") // lax.axis_size("sec") // count
    fars = count // 4
    far, pair, side = row // 4, row // 2 % 2, row % 2
    away = list(range(1, fars))
    plan = [
        (away, 1 - pair, 1 - side), ([0], 1 - pair, 1 - side), (away, pair, 1 - side), ([0], 1 - pair, side),
        (away, 1 - pair, side), ([0], pair, 1 - side), (away, pair, side), ([0], pair, side),
    ]
    where = [[((far + step) % fars * 2 + p) * 2 + s for step in steps] for steps, p, s in plan]
    lefts = (basis, moved)
    if fars == 2 and height % 128 == 0:
        size = height
        index = jnp.stack([w[0] for w in where]).astype(jnp.int32)
    else:
        size = -(-len(away) * height // 128) * 128
        index = jnp.arange(len(plan), dtype=jnp.int32)

        def gathered(left):
            columns = []
            for w in where:
                columns += [lax.dynamic_slice_in_dim(left, i * height, height, 1) for i in w]
                columns.append(jnp.zeros((rows, size - len(w) * height), left.dtype))
            return jnp.concatenate(columns, 1)

        lefts = tuple(gathered(left) for left in lefts)

    ids = tuple(x.astype(jnp.int32)[None] for x in (sec, col, row))
    tables = (neighbours, mask)
    inner, begun, ops = inner_rows(basis, own_ops, share, rest, tables, ids, lefts, index, size)
    halos = (from_before, from_after, split, swapped)
    swap_side = [(i, i ^ 1) for i in range(count)]
    swap_pair = [(i, i ^ 2) for i in range(count)]

    def rim_half(part, halos):
        rim_part, a, b = rim_rows(part, basis, halos, ops, tables, ids, lefts, index, size, begun)
        return rim_part, a[: len(away) * height], b[:height]

    def unit_half(part, which, rim_part, *dtypes):
        made = units(part, which, lefts, inner, rim_part, ids, index, size, dtypes)
        return [x[: len(plan[i][0]) * height] for i, x in zip(which, made)]

    def to_side(x):
        return lax.ppermute(x, "row", swap_side)

    def to_pair(x):
        return lax.ppermute(x, "row", swap_pair)

    def to_far(x):
        parts = []
        for i, step in enumerate(away):
            route = [(g, (g + 4 * step) % count) for g in range(count)]
            parts.append(lax.ppermute(x[i * height : (i + 1) * height], "row", route))
        return parts

    def add32(first, *others):
        for other in others:
            first = first + other.astype(F32)
        return first

    def add(first, *others):
        return add32(first, *others).astype(BF16)

    rim0, far_a0, near_a0 = rim_half(0, halos)
    far_a0, near_a0 = to_side(far_a0), to_pair(near_a0)
    far_b0, near_b0, far_c0 = unit_half(0, (2, 3, 4), rim0, BF16, BF16, F32)
    rim1, far_a1, near_a1 = rim_half(1, (after(halos[0], far_c0), *halos[1:]))
    far_b0 = to_side(far_b0)
    far_c0 = add(far_c0, after(far_a0, rim1))
    near_c0, far_d0, own0 = unit_half(0, (5, 6, 7), after(rim0, far_c0), F32, F32, F32)
    far_c0_sum = far_c0
    far_c0 = to_pair(far_c0)
    far_a1 = to_side(far_a1)
    far_b1, near_b1, far_c1 = unit_half(1, (2, 3, 4), after(rim1, own0), BF16, F32, F32)
    near_c0 = add(near_c0, after(near_a0, far_c1))
    far_b1 = to_side(far_b1)
    far_d0 = add(far_d0, after(far_b0, far_c1), far_c0)
    near_b0 = to_pair(after(near_b0, far_c0_sum))
    near_a1 = to_side(after(near_a1, far_d0))
    far_c1 = add(far_c1, after(far_a1, far_d0))
    own0 = add32(own0, after(near_b0, far_c1))
    far_d0 = to_far(far_d0)
    near_c1, far_d1, own1 = unit_half(1, (5, 6, 7), after(rim1, own0), BF16, F32, F32)
    far_c1 = to_pair(far_c1)
    near_b1 = add(near_b1, after(near_a1, far_d1))
    near_c0, near_c1 = after((near_c0, near_c1), near_b1)
    own0 = add32(own0, *after(far_d0, near_b1))
    near_b1 = to_pair(near_b1)
    far_d1 = add(far_d1, after(far_b1, own0), far_c1)
    near_c0 = to_side(near_c0)
    own0 = add32(own0, after(near_c0, far_d1))
    far_d1 = to_far(far_d1)
    own1 = add32(own1, *after(far_d1, own0))
    near_c1 = to_side(near_c1)
    near_b1, near_c1 = after((near_b1, near_c1), own1)
    return finish(((own0,), (own1, near_b1, near_c1)), 1.0 / math.sqrt(rows * count))


def solution(mesh):
    return jax.shard_map(
        per_device,
        mesh=mesh,
        in_specs=(P("row", "col"), P("row", None, "sec", None), P("row", None), P("row", None)),
        out_specs=P(("sec", "row"), "col"),
        check_vma=False,
    )
```

```python
import math

import jax
import jax.numpy as jnp
from jax import lax
from jax.experimental import pallas as pl
from jax.experimental.pallas import tpu as pltpu
from jax.sharding import PartitionSpec as P

REACH = 2
VMEM_LIMIT = 32 * 1024 * 1024
F32, BF16 = jnp.float32, jnp.bfloat16


def call(kernel, scalars, grid, in_specs, operands, out_specs, out_shape, scratch, name):
    return pl.pallas_call(
        kernel,
        grid_spec=pltpu.PrefetchScalarGridSpec(
            num_scalar_prefetch=len(scalars), grid=grid, in_specs=in_specs,
            out_specs=out_specs, scratch_shapes=scratch,
        ),
        out_shape=out_shape,
        compiler_params=pltpu.CompilerParams(vmem_limit_bytes=VMEM_LIMIT),
        cost_estimate=pl.CostEstimate(flops=1, bytes_accessed=1, transcendentals=0),
        name=name,
    )(*scalars, *operands)


def fixed(array):
    return pl.BlockSpec(array.shape, lambda j, *_: (0,) * array.ndim)


def transposed_dot(left, right):
    return lax.dot_general(left, right, (((0,), (0,)), ((), ())), preferred_element_type=F32)


def masked(b, mask_ref, halves, slots):
    rows = []
    for i in range(2):
        parts = [halves(s)[i] * mask_ref[b, s].astype(F32).astype(BF16) for s in range(slots)]
        rows.append(jnp.concatenate(parts, axis=1))
    return rows


def gathered_rows(b, shift, nb_ref, first, rows_ref, block):
    return jnp.concatenate(
        [
            rows_ref[pl.ds(pl.multiple_of((nb_ref[b, s] - first + shift) * block, block), block), :]
            for s in range(nb_ref.shape[1])
        ],
        axis=0,
    )


def inner_rows(basis, own_ops, share, rest, tables, ids, lefts, index, size):
    rows, width = basis.shape
    blocks, slots, half, block = own_ops.shape
    part, rim, tile = blocks // 2, REACH * block, width // 2

    def kernel(nb_ref, mask_ref, sec_ref, col_ref, row_ref, index_ref, rows_ref, own_ref, *refs):
        shares, rests, (m0, o0, m1, o1, out_ref, unit_ref, ops_ref) = refs[:2], refs[2:4], refs[4:]
        split = shares[0].shape[0]
        mine, sec = sec_ref[0] == col_ref[0], sec_ref[0]

        def operator(b):
            def halves(s):
                piece, at = (0, b % part) if b % part < split else (1, b % part - split)
                other = jnp.where(col_ref[0] == b // part, shares[piece][at, s], rests[piece][at, s])
                return own_ref[b, s], other

            return masked(b, mask_ref, halves, slots)

        @pl.when(pl.program_id(0) == 0)
        def _():
            for i, b in enumerate((0, 1, blocks - 2, blocks - 1)):
                own, other = operator(b)
                ops_ref[i, pl.ds(pl.multiple_of(sec * half, half), half), :] = own
                ops_ref[i, pl.ds(pl.multiple_of((1 - sec) * half, half), half), :] = other

        for b in range(REACH, blocks - REACH):
            total = jnp.dot(
                jnp.concatenate(operator(b), axis=0),
                gathered_rows(b, 0, nb_ref, row_ref[0] * blocks, rows_ref, block),
                preferred_element_type=F32,
            ).astype(BF16)
            for i, place in enumerate((sec, 1 - sec)):
                start = pl.multiple_of((b - REACH) * block + place * half, half)
                out_ref[0, pl.ds(start, half), :] = total[i * half : (i + 1) * half]
        for u, (here, there) in enumerate(((m0, o0), (m1, o1))):
            left = jnp.where(mine, here[rim : rows - rim, :], there[rim : rows - rim, :])
            unit_ref[0, u] = transposed_dot(left, out_ref[0])

    unit = [pl.BlockSpec((rows, size), lambda j, *s, u=u: (0, s[5][u])) for u in (0, 0, 1, 1)]
    ops = jax.ShapeDtypeStruct((2 * REACH, block, slots * block), BF16)
    inner = rows - 2 * rim
    return call(
        kernel, (*tables, *ids, index), (2,),
        [pl.BlockSpec((rows, tile), lambda j, *_: (0, j)), fixed(own_ops), *map(fixed, (*share, *rest))] + unit,
        (basis, own_ops, *share, *rest, *lefts, *lefts),
        [pl.BlockSpec((1, inner, tile), lambda j, *_: (j, 0, 0)),
         pl.BlockSpec((1, 2, size, tile), lambda j, *_: (j, 0, 0, 0)), fixed(ops)],
        [jax.ShapeDtypeStruct((2, inner, tile), BF16), jax.ShapeDtypeStruct((2, 2, size, tile), F32), ops],
        [], "inner_rows",
    )


def rim_rows(part, basis, halos, ops, tables, ids, lefts, index, size, begun):
    rows, width = basis.shape
    block = ops.shape[1]
    rim = REACH * block
    blocks = rows // block
    steps = 1
    tile = width // 2 // steps

    def kernel(nb_ref, mask_ref, sec_ref, col_ref, row_ref, index_ref, up_ref, down_ref, far_ref, mid_ref,
               far_swapped_ref, mid_swapped_ref, head_ref, tail0_ref, tail1_ref, ops_ref, *refs):
        left_refs, (begun_ref, out_ref, *unit_refs, ext) = refs[:8], refs[8:]
        mine, lower = sec_ref[0] == col_ref[0], sec_ref[0] == 0
        piece, direct = far_ref.shape[0], up_ref.shape[0]
        for i, (here, there) in enumerate(((far_ref, far_swapped_ref), (mid_ref, mid_swapped_ref))):
            here, there = here[...], there[...]
            ext[i * piece : (i + 1) * piece, :] = jnp.where(lower, there, here)
            end = 6 * rim - i * piece
            ext[end - piece : end, :] = jnp.where(lower, here, there)
        ext[2 * piece : rim, :] = up_ref[...]
        ext[rim : 3 * rim, :] = head_ref[...]
        ext[3 * rim : 4 * rim, :] = tail0_ref[...]
        ext[4 * rim : 5 * rim, :] = tail1_ref[...]
        ext[5 * rim : 5 * rim + direct, :] = down_ref[...]
        for i, b in enumerate((0, 1, blocks - 2, blocks - 1)):
            shift = REACH if b < REACH else 5 * REACH - blocks
            out_ref[i * block : (i + 1) * block, :] = jnp.dot(
                ops_ref[i],
                gathered_rows(b, shift, nb_ref, row_ref[0] * blocks, ext, block),
                preferred_element_type=F32,
            ).astype(BF16)
        for u, unit_ref in enumerate(unit_refs):
            total = begun_ref[0, u]
            for i in range(2):
                here, there = left_refs[4 * u + 2 * i : 4 * u + 2 * i + 2]
                left = jnp.where(mine, here[...], there[...])
                total = total + transposed_dot(left, out_ref[i * rim : (i + 1) * rim, :])
            unit_ref[...] = total.astype(BF16)

    last = rows // rim - 1
    unit = [
        pl.BlockSpec((rim, size), lambda j, *s, u=u, at=at: (at, s[5][u]))
        for u in range(2) for at in (0, last) for _ in range(2)
    ]

    def across(height, at=0):
        return pl.BlockSpec((height, tile), lambda j, *_: (at, part * steps + j))

    def out(height):
        return pl.BlockSpec((height, tile), lambda j, *_: (0, j))

    return call(
        kernel, (*tables, *ids, index), (steps,),
        [across(x.shape[0]) for x in halos] + [across(2 * rim), across(rim, last - 1), across(rim, last), fixed(ops)]
        + unit + [pl.BlockSpec((1, 2, size, tile), lambda j, *_: (part, 0, 0, j))],
        (*halos, basis, basis, basis, ops, *(lefts * 4), begun),
        [out(2 * rim), out(size), out(size)],
        [jax.ShapeDtypeStruct((2 * rim, width // 2), BF16)]
        + [jax.ShapeDtypeStruct((size, width // 2), BF16)] * 2,
        [pltpu.VMEM((6 * rim, tile), BF16)], "rim_rows",
    )


def units(part, which, lefts, inner, rim_part, ids, index, size, dtypes):
    rows = lefts[0].shape[0]
    width = inner.shape[2]
    rim = rim_part.shape[0] // 2
    first, count = which[0], len(which)
    assert list(which) == list(range(first, first + count))

    def kernel(sec_ref, col_ref, row_ref, index_ref, here, there, inner_ref, rim_ref, *out_refs):
        left = jnp.where(sec_ref[0] == col_ref[0], here[...], there[...])
        total = (
            transposed_dot(left[rim : rows - rim], inner_ref[0])
            + transposed_dot(left[:rim], rim_ref[:rim, :])
            + transposed_dot(left[rows - rim :], rim_ref[rim:, :])
        )
        for u, out_ref in enumerate(out_refs):
            @pl.when(pl.program_id(0) == u)
            def _(out_ref=out_ref):
                out_ref[...] = total.astype(out_ref.dtype)

    unit = pl.BlockSpec((rows, size), lambda u, *s: (0, s[3][first + u]))
    return call(
        kernel, (*ids, index), (count,),
        [unit, unit, pl.BlockSpec((1, *inner.shape[1:]), lambda u, *_: (part, 0, 0)), fixed(rim_part)],
        (*lefts, inner, rim_part),
        [pl.BlockSpec((size, width), lambda u, *_: (0, 0))] * count,
        [jax.ShapeDtypeStruct((size, width), dtype) for dtype in dtypes], [], "units",
    )


def finish(halves, scale):
    height, width = halves[0][0].shape
    count = len(halves[0])

    def kernel(*refs):
        for part, chosen in enumerate((refs[:count], refs[count:-1])):
            @pl.when(pl.program_id(0) == part)
            def _(chosen=chosen):
                total = chosen[0][...]
                for ref in chosen[1:]:
                    total = total + ref[...].astype(F32)
                refs[-1][...] = total * scale

    operands = [x for half in halves for x in half]
    return call(
        kernel, (), (2,), [fixed(x) for x in operands], operands,
        pl.BlockSpec((height, width), lambda j: (0, j)),
        jax.ShapeDtypeStruct((height, 2 * width), F32), [], "finish",
    )


def per_device(basis, own_ops, neighbours, mask):
    rows, width = basis.shape
    blocks, slots, half, block = own_ops.shape
    sec, row, col = (lax.axis_index(name) for name in ("sec", "row", "col"))
    count = lax.axis_size("row")
    rim = REACH * block
    swap = [(0, 1), (1, 0)]
    up = [(i, (i + 1) % count) for i in range(count)]
    down = [(j, i) for i, j in up]

    def after(value, *earlier):
        return lax.optimization_barrier((value, earlier))[0]

    direct = rim * 4 // 8
    piece = (rim - direct) // 2
    split = [
        lax.dynamic_slice_in_dim(basis, near + sec * (rows - rim + i * piece - near), piece, 0)
        for i, near in enumerate((direct + piece, direct))
    ]
    behind = after(basis, split)
    inward = down + [(count + i, count + j) for i, j in up]
    split = [lax.ppermute(x, ("sec", "row"), inward) for x in split]
    part = blocks // 2
    cuts = (0, part // 2, part)
    share = [
        lax.dynamic_slice_in_dim(own_ops, col * part + i, j - i, 0) for i, j in zip(cuts, cuts[1:])
    ]
    behind = after(behind, share)
    share = [lax.ppermute(x, "sec", swap) for x in share]
    from_before = lax.ppermute(behind[rows - direct :], "row", up)
    from_after = lax.ppermute(behind[:direct], "row", down)
    moved = lax.ppermute(behind, "col", swap)
    rest = [lax.ppermute(x, "col", swap) for x in share]
    swapped = [lax.ppermute(after(x, moved), "sec", swap) for x in split]

    height = width * lax.axis_size("col") // lax.axis_size("sec") // count
    fars = count // 4
    far, pair, side = row // 4, row // 2 % 2, row % 2
    away = list(range(1, fars))
    plan = [
        (away, 1 - pair, 1 - side), ([0], 1 - pair, 1 - side), (away, pair, 1 - side), (away, 1 - pair, side),
        ([0], 1 - pair, side), ([0], pair, 1 - side), (away, pair, side), ([0], pair, side),
    ]
    where = [[((far + step) % fars * 2 + p) * 2 + s for step in steps] for steps, p, s in plan]
    lefts = (basis, moved)
    if fars == 2 and height % 128 == 0:
        size = height
        index = jnp.stack([w[0] for w in where]).astype(jnp.int32)
    else:
        size = -(-len(away) * height // 128) * 128
        index = jnp.arange(len(plan), dtype=jnp.int32)

        def gathered(left):
            columns = []
            for w in where:
                columns += [lax.dynamic_slice_in_dim(left, i * height, height, 1) for i in w]
                columns.append(jnp.zeros((rows, size - len(w) * height), left.dtype))
            return jnp.concatenate(columns, 1)

        lefts = tuple(gathered(left) for left in lefts)

    ids = tuple(x.astype(jnp.int32)[None] for x in (sec, col, row))
    tables = (neighbours, mask)
    inner, begun, ops = inner_rows(basis, own_ops, share, rest, tables, ids, lefts, index, size)
    halos = (from_before, from_after, *split, *swapped)
    swap_side = [(i, i ^ 1) for i in range(count)]
    swap_pair = [(i, i ^ 2) for i in range(count)]

    def rim_half(part, halos):
        rim_part, a, b = rim_rows(part, basis, halos, ops, tables, ids, lefts, index, size, begun)
        return rim_part, a[: len(away) * height], b[:height]

    def unit_half(part, which, rim_part, *dtypes):
        made = units(part, which, lefts, inner, rim_part, ids, index, size, dtypes)
        return [x[: len(plan[i][0]) * height] for i, x in zip(which, made)]

    def to_side(x):
        return lax.ppermute(x, "row", swap_side)

    def to_pair(x):
        return lax.ppermute(x, "row", swap_pair)

    def to_far(x):
        parts = []
        for i, step in enumerate(away):
            route = [(g, (g + 4 * step) % count) for g in range(count)]
            parts.append(lax.ppermute(x[i * height : (i + 1) * height], "row", route))
        return parts

    def add32(first, *others):
        for other in others:
            first = first + other.astype(F32)
        return first

    def add(first, *others):
        return add32(first, *others).astype(BF16)

    rim0, far_a0, near_a0 = rim_half(0, halos)
    far_a0, near_a0 = to_side(far_a0), to_pair(near_a0)
    far_b0, far_c0 = unit_half(0, (2, 3), rim0, BF16, F32)
    rim1, far_a1, near_a1 = rim_half(1, (after(halos[0], far_c0), *halos[1:]))
    far_b0 = to_side(far_b0)
    far_c0 = add(far_c0, after(far_a0, rim1))
    near_b0, near_c0, far_d0, own0 = unit_half(
        0, (4, 5, 6, 7), after(rim0, far_c0), BF16, F32, F32, F32
    )
    far_c0_sum = far_c0
    far_c0 = to_pair(far_c0)
    far_a1 = to_side(far_a1)
    far_b1, far_c1 = unit_half(1, (2, 3), after(rim1, own0), BF16, F32)
    near_c0 = add(near_c0, after(near_a0, far_c1))
    far_b1 = to_side(far_b1)
    far_d0 = add(far_d0, after(far_b0, far_c1), far_c0)
    near_b0 = to_pair(near_b0)
    near_a1 = to_side(after(near_a1, far_d0))
    far_c1 = add(far_c1, after(far_a1, far_d0))
    own0 = add32(own0, after(near_b0, far_c1))
    far_d0 = to_far(far_d0)
    near_b1, near_c1, far_d1, own1 = unit_half(
        1, (4, 5, 6, 7), after(rim1, own0), F32, BF16, F32, F32
    )
    far_c1 = to_pair(far_c1)
    near_b1 = add(near_b1, after(near_a1, far_d1))
    near_c0, near_c1 = after((near_c0, near_c1), near_b1)
    own0 = add32(own0, *after(far_d0, near_b1))
    near_b1 = to_pair(near_b1)
    far_d1 = add(far_d1, after(far_b1, own0), far_c1)
    near_c0 = to_side(near_c0)
    own0 = add32(own0, after(near_c0, far_d1))
    far_d1 = to_far(far_d1)
    own1 = add32(own1, *after(far_d1, own0))
    near_c1 = to_side(near_c1)
    near_b1, near_c1 = after((near_b1, near_c1), own1)
    return finish(((own0,), (own1, near_b1, near_c1)), 1.0 / math.sqrt(rows * count))


def solution(mesh):
    return jax.shard_map(
        per_device,
        mesh=mesh,
        in_specs=(P("row", "col"), P("row", None, "sec", None), P("row", None), P("row", None)),
        out_specs=P(("sec", "row"), "col"),
        check_vma=False,
    )
```

```python
import math

import jax
import jax.numpy as jnp
from jax import lax
from jax.experimental import pallas as pl
from jax.experimental.pallas import tpu as pltpu
from jax.sharding import PartitionSpec as P

REACH = 2
VMEM_LIMIT = 32 * 1024 * 1024
F32, BF16 = jnp.float32, jnp.bfloat16


def call(kernel, scalars, grid, in_specs, operands, out_specs, out_shape, scratch, name):
    return pl.pallas_call(
        kernel,
        grid_spec=pltpu.PrefetchScalarGridSpec(
            num_scalar_prefetch=len(scalars), grid=grid, in_specs=in_specs,
            out_specs=out_specs, scratch_shapes=scratch,
        ),
        out_shape=out_shape,
        compiler_params=pltpu.CompilerParams(vmem_limit_bytes=VMEM_LIMIT),
        cost_estimate=pl.CostEstimate(flops=1, bytes_accessed=1, transcendentals=0),
        name=name,
    )(*scalars, *operands)


def fixed(array):
    return pl.BlockSpec(array.shape, lambda j, *_: (0,) * array.ndim)


def transposed_dot(left, right):
    return lax.dot_general(left, right, (((0,), (0,)), ((), ())), preferred_element_type=F32)


def masked(b, mask_ref, halves, slots):
    rows = []
    for i in range(2):
        parts = [halves(s)[i] * mask_ref[b, s].astype(F32).astype(BF16) for s in range(slots)]
        rows.append(jnp.concatenate(parts, axis=1))
    return rows


def gathered_rows(b, shift, nb_ref, first, rows_ref, block):
    return jnp.concatenate(
        [
            rows_ref[pl.ds(pl.multiple_of((nb_ref[b, s] - first + shift) * block, block), block), :]
            for s in range(nb_ref.shape[1])
        ],
        axis=0,
    )


def inner_rows(basis, own_ops, share, rest, tables, ids, lefts, index, size):
    rows, width = basis.shape
    blocks, slots, half, block = own_ops.shape
    part, rim, tile = blocks // 2, REACH * block, width // 2

    def kernel(nb_ref, mask_ref, sec_ref, col_ref, row_ref, index_ref, rows_ref, own_ref, *refs):
        shares, rests, (m0, o0, m1, o1, out_ref, unit_ref, ops_ref) = refs[:2], refs[2:4], refs[4:]
        split = shares[0].shape[0]
        mine, sec = sec_ref[0] == col_ref[0], sec_ref[0]

        def operator(b):
            def halves(s):
                piece, at = (0, b % part) if b % part < split else (1, b % part - split)
                other = jnp.where(col_ref[0] == b // part, shares[piece][at, s], rests[piece][at, s])
                return own_ref[b, s], other

            return masked(b, mask_ref, halves, slots)

        @pl.when(pl.program_id(0) == 0)
        def _():
            for i, b in enumerate((0, 1, blocks - 2, blocks - 1)):
                own, other = operator(b)
                ops_ref[i, pl.ds(pl.multiple_of(sec * half, half), half), :] = own
                ops_ref[i, pl.ds(pl.multiple_of((1 - sec) * half, half), half), :] = other

        for b in range(REACH, blocks - REACH):
            total = jnp.dot(
                jnp.concatenate(operator(b), axis=0),
                gathered_rows(b, 0, nb_ref, row_ref[0] * blocks, rows_ref, block),
                preferred_element_type=F32,
            ).astype(BF16)
            for i, place in enumerate((sec, 1 - sec)):
                start = pl.multiple_of((b - REACH) * block + place * half, half)
                out_ref[0, pl.ds(start, half), :] = total[i * half : (i + 1) * half]
        for u, (here, there) in enumerate(((m0, o0), (m1, o1))):
            left = jnp.where(mine, here[rim : rows - rim, :], there[rim : rows - rim, :])
            unit_ref[0, u] = transposed_dot(left, out_ref[0])

    unit = [pl.BlockSpec((rows, size), lambda j, *s, u=u: (0, s[5][u])) for u in (0, 0, 1, 1)]
    ops = jax.ShapeDtypeStruct((2 * REACH, block, slots * block), BF16)
    inner = rows - 2 * rim
    return call(
        kernel, (*tables, *ids, index), (2,),
        [pl.BlockSpec((rows, tile), lambda j, *_: (0, j)), fixed(own_ops), *map(fixed, (*share, *rest))] + unit,
        (basis, own_ops, *share, *rest, *lefts, *lefts),
        [pl.BlockSpec((1, inner, tile), lambda j, *_: (j, 0, 0)),
         pl.BlockSpec((1, 2, size, tile), lambda j, *_: (j, 0, 0, 0)), fixed(ops)],
        [jax.ShapeDtypeStruct((2, inner, tile), BF16), jax.ShapeDtypeStruct((2, 2, size, tile), F32), ops],
        [], "inner_rows",
    )


def rim_rows(part, basis, halos, ops, tables, ids, lefts, index, size, begun):
    rows, width = basis.shape
    block = ops.shape[1]
    rim = REACH * block
    blocks = rows // block
    steps = 1
    tile = width // 2 // steps

    def kernel(nb_ref, mask_ref, sec_ref, col_ref, row_ref, index_ref, up_ref, down_ref, far_ref, mid_ref,
               far_swapped_ref, mid_swapped_ref, head_ref, tail0_ref, tail1_ref, ops_ref, *refs):
        left_refs, (begun_ref, out_ref, *unit_refs, ext) = refs[:8], refs[8:]
        mine, lower = sec_ref[0] == col_ref[0], sec_ref[0] == 0
        piece, direct = far_ref.shape[0], up_ref.shape[0]
        for i, (here, there) in enumerate(((far_ref, far_swapped_ref), (mid_ref, mid_swapped_ref))):
            here, there = here[...], there[...]
            ext[i * piece : (i + 1) * piece, :] = jnp.where(lower, there, here)
            end = 6 * rim - i * piece
            ext[end - piece : end, :] = jnp.where(lower, here, there)
        ext[2 * piece : rim, :] = up_ref[...]
        ext[rim : 3 * rim, :] = head_ref[...]
        ext[3 * rim : 4 * rim, :] = tail0_ref[...]
        ext[4 * rim : 5 * rim, :] = tail1_ref[...]
        ext[5 * rim : 5 * rim + direct, :] = down_ref[...]
        for i, b in enumerate((0, 1, blocks - 2, blocks - 1)):
            shift = REACH if b < REACH else 5 * REACH - blocks
            out_ref[i * block : (i + 1) * block, :] = jnp.dot(
                ops_ref[i],
                gathered_rows(b, shift, nb_ref, row_ref[0] * blocks, ext, block),
                preferred_element_type=F32,
            ).astype(BF16)
        for u, unit_ref in enumerate(unit_refs):
            total = begun_ref[0, u]
            for i in range(2):
                here, there = left_refs[4 * u + 2 * i : 4 * u + 2 * i + 2]
                left = jnp.where(mine, here[...], there[...])
                total = total + transposed_dot(left, out_ref[i * rim : (i + 1) * rim, :])
            unit_ref[...] = total.astype(BF16)

    last = rows // rim - 1
    unit = [
        pl.BlockSpec((rim, size), lambda j, *s, u=u, at=at: (at, s[5][u]))
        for u in range(2) for at in (0, last) for _ in range(2)
    ]

    def across(height, at=0):
        return pl.BlockSpec((height, tile), lambda j, *_: (at, part * steps + j))

    def out(height):
        return pl.BlockSpec((height, tile), lambda j, *_: (0, j))

    return call(
        kernel, (*tables, *ids, index), (steps,),
        [across(x.shape[0]) for x in halos] + [across(2 * rim), across(rim, last - 1), across(rim, last), fixed(ops)]
        + unit + [pl.BlockSpec((1, 2, size, tile), lambda j, *_: (part, 0, 0, j))],
        (*halos, basis, basis, basis, ops, *(lefts * 4), begun),
        [out(2 * rim), out(size), out(size)],
        [jax.ShapeDtypeStruct((2 * rim, width // 2), BF16)]
        + [jax.ShapeDtypeStruct((size, width // 2), BF16)] * 2,
        [pltpu.VMEM((6 * rim, tile), BF16)], "rim_rows",
    )


def units(part, which, lefts, inner, rim_part, ids, index, size, dtypes):
    rows = lefts[0].shape[0]
    width = inner.shape[2]
    rim = rim_part.shape[0] // 2
    first, count = which[0], len(which)
    assert list(which) == list(range(first, first + count))

    def kernel(sec_ref, col_ref, row_ref, index_ref, here, there, inner_ref, rim_ref, *out_refs):
        left = jnp.where(sec_ref[0] == col_ref[0], here[...], there[...])
        total = (
            transposed_dot(left[rim : rows - rim], inner_ref[0])
            + transposed_dot(left[:rim], rim_ref[:rim, :])
            + transposed_dot(left[rows - rim :], rim_ref[rim:, :])
        )
        for u, out_ref in enumerate(out_refs):
            @pl.when(pl.program_id(0) == u)
            def _(out_ref=out_ref):
                out_ref[...] = total.astype(out_ref.dtype)

    unit = pl.BlockSpec((rows, size), lambda u, *s: (0, s[3][first + u]))
    return call(
        kernel, (*ids, index), (count,),
        [unit, unit, pl.BlockSpec((1, *inner.shape[1:]), lambda u, *_: (part, 0, 0)), fixed(rim_part)],
        (*lefts, inner, rim_part),
        [pl.BlockSpec((size, width), lambda u, *_: (0, 0))] * count,
        [jax.ShapeDtypeStruct((size, width), dtype) for dtype in dtypes], [], "units",
    )


def finish(halves, scale):
    height, width = halves[0][0].shape
    count = len(halves[0])

    def kernel(*refs):
        for part, chosen in enumerate((refs[:count], refs[count:-1])):
            @pl.when(pl.program_id(0) == part)
            def _(chosen=chosen):
                total = chosen[0][...]
                for ref in chosen[1:]:
                    total = total + ref[...].astype(F32)
                refs[-1][...] = total * scale

    operands = [x for half in halves for x in half]
    return call(
        kernel, (), (2,), [fixed(x) for x in operands], operands,
        pl.BlockSpec((height, width), lambda j: (0, j)),
        jax.ShapeDtypeStruct((height, 2 * width), F32), [], "finish",
    )


def per_device(basis, own_ops, neighbours, mask):
    rows, width = basis.shape
    blocks, slots, half, block = own_ops.shape
    sec, row, col = (lax.axis_index(name) for name in ("sec", "row", "col"))
    count = lax.axis_size("row")
    rim = REACH * block
    swap = [(0, 1), (1, 0)]
    up = [(i, (i + 1) % count) for i in range(count)]
    down = [(j, i) for i, j in up]

    def after(value, *earlier):
        return lax.optimization_barrier((value, earlier))[0]

    direct = rim * 4 // 8
    piece = (rim - direct) // 2
    split = [
        lax.dynamic_slice_in_dim(basis, near + sec * (rows - rim + i * piece - near), piece, 0)
        for i, near in enumerate((direct + piece, direct))
    ]
    behind = after(basis, split)
    inward = down + [(count + i, count + j) for i, j in up]
    split = [lax.ppermute(x, ("sec", "row"), inward) for x in split]
    part = blocks // 2
    cuts = (0, part // 2, part)
    share = [
        lax.dynamic_slice_in_dim(own_ops, col * part + i, j - i, 0) for i, j in zip(cuts, cuts[1:])
    ]
    behind = after(behind, share)
    share = [lax.ppermute(x, "sec", swap) for x in share]
    nearby = after(behind, split[1])
    from_before = lax.ppermute(nearby[rows - direct :], "row", up)
    from_after = lax.ppermute(nearby[:direct], "row", down)
    moved = lax.ppermute(behind, "col", swap)
    rest = [lax.ppermute(x, "col", swap) for x in share]
    swapped = [lax.ppermute(after(x, moved), "sec", swap) for x in split]

    height = width * lax.axis_size("col") // lax.axis_size("sec") // count
    fars = count // 4
    far, pair, side = row // 4, row // 2 % 2, row % 2
    away = list(range(1, fars))
    plan = [
        (away, 1 - pair, 1 - side), ([0], 1 - pair, 1 - side), (away, pair, 1 - side), (away, 1 - pair, side),
        ([0], 1 - pair, side), ([0], pair, 1 - side), (away, pair, side), ([0], pair, side),
    ]
    where = [[((far + step) % fars * 2 + p) * 2 + s for step in steps] for steps, p, s in plan]
    lefts = (basis, moved)
    if fars == 2 and height % 128 == 0:
        size = height
        index = jnp.stack([w[0] for w in where]).astype(jnp.int32)
    else:
        size = -(-len(away) * height // 128) * 128
        index = jnp.arange(len(plan), dtype=jnp.int32)

        def gathered(left):
            columns = []
            for w in where:
                columns += [lax.dynamic_slice_in_dim(left, i * height, height, 1) for i in w]
                columns.append(jnp.zeros((rows, size - len(w) * height), left.dtype))
            return jnp.concatenate(columns, 1)

        lefts = tuple(gathered(left) for left in lefts)

    ids = tuple(x.astype(jnp.int32)[None] for x in (sec, col, row))
    tables = (neighbours, mask)
    inner, begun, ops = inner_rows(basis, own_ops, share, rest, tables, ids, lefts, index, size)
    halos = (from_before, from_after, *split, *swapped)
    swap_side = [(i, i ^ 1) for i in range(count)]
    swap_pair = [(i, i ^ 2) for i in range(count)]

    def rim_half(part, halos):
        rim_part, a, b = rim_rows(part, basis, halos, ops, tables, ids, lefts, index, size, begun)
        return rim_part, a[: len(away) * height], b[:height]

    def unit_half(part, which, rim_part, *dtypes):
        made = units(part, which, lefts, inner, rim_part, ids, index, size, dtypes)
        return [x[: len(plan[i][0]) * height] for i, x in zip(which, made)]

    def to_side(x):
        return lax.ppermute(x, "row", swap_side)

    def to_pair(x):
        return lax.ppermute(x, "row", swap_pair)

    def to_far(x):
        parts = []
        for i, step in enumerate(away):
            route = [(g, (g + 4 * step) % count) for g in range(count)]
            parts.append(lax.ppermute(x[i * height : (i + 1) * height], "row", route))
        return parts

    def add32(first, *others):
        for other in others:
            first = first + other.astype(F32)
        return first

    def add(first, *others):
        return add32(first, *others).astype(BF16)

    rim0, far_a0, near_a0 = rim_half(0, halos)
    far_a0, near_a0 = to_side(far_a0), to_pair(near_a0)
    far_b0, far_c0 = unit_half(0, (2, 3), rim0, BF16, F32)
    rim1, far_a1, near_a1 = rim_half(1, (after(halos[0], far_c0), *halos[1:]))
    far_b0 = to_side(far_b0)
    far_c0 = add(far_c0, after(far_a0, rim1))
    near_b0, near_c0, far_d0, own0 = unit_half(
        0, (4, 5, 6, 7), after(rim0, far_c0), BF16, F32, F32, F32
    )
    far_c0_sum = far_c0
    far_c0 = to_pair(far_c0)
    far_a1 = to_side(far_a1)
    far_b1, far_c1 = unit_half(1, (2, 3), after(rim1, own0), BF16, F32)
    near_c0 = add(near_c0, after(near_a0, far_c1))
    far_b1 = to_side(far_b1)
    far_d0 = add(far_d0, after(far_b0, far_c1), far_c0)
    near_b0 = to_pair(near_b0)
    near_a1 = to_side(after(near_a1, far_d0))
    far_c1 = add(far_c1, after(far_a1, far_d0))
    own0 = add32(own0, after(near_b0, far_c1))
    far_d0 = to_far(far_d0)
    near_b1, near_c1, far_d1, own1 = unit_half(
        1, (4, 5, 6, 7), after(rim1, own0), F32, BF16, F32, F32
    )
    far_c1 = to_pair(far_c1)
    near_b1 = add(near_b1, after(near_a1, far_d1))
    near_c0, near_c1 = after((near_c0, near_c1), near_b1)
    own0 = add32(own0, *after(far_d0, near_b1))
    near_b1 = to_pair(near_b1)
    far_d1 = add(far_d1, after(far_b1, own0), far_c1)
    near_c0 = to_side(near_c0)
    own0 = add32(own0, after(near_c0, far_d1))
    far_d1 = to_far(far_d1)
    own1 = add32(own1, *after(far_d1, own0))
    near_c1 = to_side(near_c1)
    near_b1, near_c1 = after((near_b1, near_c1), own1)
    return finish(((own0,), (own1, near_b1, near_c1)), 1.0 / math.sqrt(rows * count))


def solution(mesh):
    return jax.shard_map(
        per_device,
        mesh=mesh,
        in_specs=(P("row", "col"), P("row", None, "sec", None), P("row", None), P("row", None)),
        out_specs=P(("sec", "row"), "col"),
        check_vma=False,
    )
```
